128 devices in a mesh: section: 2 (over core), seq: 4 (over x), wa: 16 (over z, y).
Axes of the slice: x: 4, y: 4, z: 4, core: 2. Of those that a mesh axis runs over, the one named last changes fastest.
Arguments:
- tokens: bfloat16 [4, 1024, 1024], P(None, 'seq'), may hold values from -6 to 6
- cotangent: float32 [4, 1024, 1024], P(None, 'seq'), may hold values from -6 to 6
- in_weight: bfloat16 [2, 1024, 3, 1024], P('section', None, None, 'wa'), may hold values from -0.1875 to 0.1875
- conv_weight: float32 [2, 3, 1024], P('section', None, 'wa'), may hold values from -3 to 3
- out_weight: bfloat16 [2, 1024, 1024], P('section', 'wa'), may hold values from -0.1875 to 0.1875
- norm_gain: float32 [2, 1024], P('section'), may hold values from 0.25 to 1.75
- gate_up_weight: bfloat16 [2, 1024, 2, 4608], P('section', None, None, 'wa'), may hold values from -0.1875 to 0.1875
- down_weight: bfloat16 [2, 4608, 1024], P('section', 'wa'), may hold values from -0.09375 to 0.09375
Outputs:
- layer_out: bfloat16 [2, 4, 1024, 1024], P('section', None, ('seq', 'wa'))
- input_grad: float32 [2, 4, 1024, 1024], P('section', None, ('seq', 'wa'))
- in_weight_grad: float32 [2, 1024, 3, 1024], P('section', None, None, 'wa')
- conv_weight_grad: float32 [2, 3, 1024], P('section', None, 'wa')
- out_weight_grad: float32 [2, 1024, 1024], P('section', 'wa')
- norm_gain_grad: float32 [2, 1024], P('section')
- gate_up_grad: float32 [2, 1024, 2, 4608], P('section', None, None, 'wa')
- down_grad: float32 [2, 4608, 1024], P('section', 'wa')
The draws below stay inside these ranges and needn't reach their ends.
All inputs are finite; a program needn't handle non-finite values.
Results may differ from the reference program's by a relative error of at most 0.025.
Values may be sent and summed in bfloat16 or wider, within the bound.
A program may use at most 128 MiB of HBM per device.

```python
import jax
import jax.numpy as jnp
from jax import lax

D = 1024
FF = 4608
MICRO = 4
SEQ_TOK = 1024


def block_levels(key, dims, pieces, smallest, top_value):
    def one(dim, shards_of):
        heights = jax.random.uniform(jax.random.fold_in(jax.random.fold_in(key, 6), dim), (shards_of,), jnp.float32, smallest / len(pieces), top_value / len(pieces))
        return jnp.repeat(jnp.exp(heights), dims[dim] // shards_of).reshape((-1,) + (1,) * (len(dims) - dim - 1))

    gain = one(*pieces[0])
    for cut in pieces[1:]:
        gain = gain * one(*cut)
    return gain


def noise(rng, extent, spread, most, shards=(), dtype=jnp.bfloat16):
    array = spread * jax.random.normal(rng, extent, jnp.float32)
    if shards:
        array = array * block_levels(rng, extent, shards, -0.22, 0.18)
    return jnp.clip(array, -most, most).astype(dtype)


def setup_inputs(seed: int = 0) -> dict:
    splits = jax.random.split(jax.random.key(seed), 9)
    tokens = noise(splits[0], (MICRO, SEQ_TOK, D), 1.0, 6.0, ((1, 4),))
    cotangent = noise(splits[1], (MICRO, SEQ_TOK, D), 1.0, 6.0, ((1, 4),), jnp.float32)
    in_weight = noise(splits[2], (2, D, 3, D), D ** -0.5, 0.1875, ((0, 2), (3, 16)))
    conv_weight = noise(splits[3], (2, 3, D), 0.6, 3.0, ((0, 2), (2, 16)), jnp.float32)
    out_weight = noise(splits[4], (2, D, D), D ** -0.5, 0.1875, ((0, 2), (1, 16)))
    norm_gain = jnp.clip(1.0 + 0.15 * jax.random.normal(splits[5], (2, D), jnp.float32), 0.25, 1.75)
    gate_up_weight = noise(splits[6], (2, D, 2, FF), D ** -0.5, 0.1875, ((0, 2), (3, 16)))
    down_weight = noise(splits[7], (2, FF, D), FF ** -0.5, 0.09375, ((0, 2), (1, 16)))
    return {"tokens": tokens, "cotangent": cotangent, "in_weight": in_weight, "conv_weight": conv_weight, "out_weight": out_weight, "norm_gain": norm_gain, "gate_up_weight": gate_up_weight, "down_weight": down_weight}


EPSILON = 1e-05

def contract_first(lhs_matrix, rhs_matrix):
    return lax.dot_general(lhs_matrix, rhs_matrix, (((0,), (0,)), ((), ())), preferred_element_type=jnp.float32)

def contract_last(lhs_matrix, rhs_matrix):
    return lax.dot_general(lhs_matrix, rhs_matrix, (((1,), (1,)), ((), ())), preferred_element_type=jnp.float32)

def silu_parts(gate_val):
    sigmoid_val = jax.nn.sigmoid(gate_val)
    return (gate_val * sigmoid_val, sigmoid_val * (1.0 + gate_val * (1.0 - sigmoid_val)))

def layer_forward(inputs, params):
    in_matrix, conv_taps, out_matrix, gain_row, gate_up, down_matrix = params
    length, model_width = inputs.shape
    hidden_width = gate_up.shape[2]
    projected = jnp.dot(inputs, in_matrix.reshape(model_width, -1), preferred_element_type=jnp.float32).reshape(length, 3, model_width)
    gated_in = (projected[:, 0] * projected[:, 2]).astype(jnp.bfloat16)
    padded = jnp.concatenate([jnp.zeros((2, model_width), jnp.bfloat16), gated_in], 0).astype(jnp.float32)
    conv_out = conv_taps[0] * padded[:length] + conv_taps[1] * padded[1:length + 1] + conv_taps[2] * padded[2:]
    mixed_in = (projected[:, 1] * conv_out).astype(jnp.bfloat16)
    residual = inputs.astype(jnp.float32) + jnp.dot(mixed_in, out_matrix, preferred_element_type=jnp.float32)
    inv_rms = lax.rsqrt(lax.optimization_barrier(jnp.mean(residual * residual, -1, keepdims=True)) + EPSILON)
    normed = (residual * inv_rms * gain_row).astype(jnp.bfloat16)
    gate_up_val = jnp.dot(normed, gate_up.reshape(model_width, -1), preferred_element_type=jnp.float32).reshape(length, 2, hidden_width)
    gate_val = gate_up_val[:, 0]
    up_val = gate_up_val[:, 1]
    hidden = (silu_parts(gate_val)[0] * up_val).astype(jnp.bfloat16)
    layer_rows = (residual + jnp.dot(hidden, down_matrix, preferred_element_type=jnp.float32)).astype(jnp.bfloat16)
    return (layer_rows, (projected, padded, conv_out, mixed_in, residual, inv_rms, normed, gate_val, up_val, hidden))

def layer_backward(out_grad, inputs, kept, params):
    in_matrix, conv_taps, out_matrix, gain_row, gate_up, down_matrix = params
    projected, padded, conv_out, mixed_in, residual, inv_rms, normed, gate_val, up_val, hidden = kept
    length, model_width = inputs.shape
    hidden_width = gate_up.shape[2]
    out_bf = out_grad.astype(jnp.bfloat16)
    hidden_grad = contract_last(out_bf, down_matrix)
    silu_val, silu_slope = silu_parts(gate_val)
    gate_up_bf = jnp.stack([hidden_grad * up_val * silu_slope, hidden_grad * silu_val], 1).astype(jnp.bfloat16).reshape(length, 2 * hidden_width)
    normed_grad = contract_last(gate_up_bf, gate_up.reshape(model_width, -1))
    scaled_grad = normed_grad * gain_row
    gain_grad = lax.optimization_barrier(jnp.sum(normed_grad * residual * inv_rms, 0))
    residual_grad = out_grad + inv_rms * scaled_grad - residual * inv_rms ** 3 * lax.optimization_barrier(jnp.mean(scaled_grad * residual, -1, keepdims=True))
    residual_bf = residual_grad.astype(jnp.bfloat16)
    mixed_grad = contract_last(residual_bf, out_matrix)
    c_grad = mixed_grad * conv_out
    conv_grad = mixed_grad * projected[:, 1]
    extended = jnp.concatenate([conv_grad, jnp.zeros((2, model_width), jnp.float32)], 0)
    gated_grad = conv_taps[2] * extended[:length] + conv_taps[1] * extended[1:length + 1] + conv_taps[0] * extended[2:]
    tap_grad = jnp.stack([lax.optimization_barrier(jnp.sum(conv_grad * padded[offset:offset + length], 0)) for offset in range(3)])
    proj_bf = jnp.stack([gated_grad * projected[:, 2], c_grad, gated_grad * projected[:, 0]], 1).astype(jnp.bfloat16).reshape(length, 3 * model_width)
    input_rows = residual_grad + contract_last(proj_bf, in_matrix.reshape(model_width, -1))
    grads = (contract_first(inputs, proj_bf).reshape(model_width, 3, model_width), tap_grad, contract_first(mixed_in, residual_bf), gain_grad, contract_first(normed, gate_up_bf).reshape(model_width, 2, hidden_width), contract_first(hidden, out_bf))
    return (input_rows, grads)

def reference(tokens, cotangent, in_weight, conv_weight, out_weight, norm_gain, gate_up_weight, down_weight):
    micro_count, seq_rows, model_width = tokens.shape
    params_first = (in_weight[0], conv_weight[0], out_weight[0], norm_gain[0], gate_up_weight[0], down_weight[0])
    params_second = (in_weight[1], conv_weight[1], out_weight[1], norm_gain[1], gate_up_weight[1], down_weight[1])
    first_in = tokens.reshape(-1, model_width)
    first_out, kept_first = layer_forward(first_in, params_first)
    second_out, kept_second = layer_forward(first_out, params_second)
    second_grad, grads_second = layer_backward(cotangent.reshape(-1, model_width), first_out, kept_second, params_second)
    first_grad, grads_first = layer_backward(second_grad, first_in, kept_first, params_first)
    layer_out = jnp.stack([first_out, second_out]).reshape(2, micro_count, seq_rows, model_width)
    input_grad = jnp.stack([first_grad, second_grad]).reshape(2, micro_count, seq_rows, model_width)
    stacked = [jnp.stack([grads_first[number], grads_second[number]]) for number in range(6)]
    return (layer_out, input_grad, stacked[0], stacked[1], stacked[2], stacked[3], stacked[4], stacked[5])
```

```python
import functools
import types

import jax
import jax.numpy as jnp
from jax import lax
from jax.experimental import pallas as pl
from jax.experimental.pallas import tpu as pltpu
from jax.sharding import PartitionSpec as P

EPSILON = 1e-05
MESH = pl.DeviceIdType.MESH
BF = jnp.bfloat16
F32 = jnp.float32
ROWS = 16
CHUNKS = 2


def dot_nn(a, b):
    return jnp.dot(a, b, preferred_element_type=F32)


def dot_nt(a, b):
    return lax.dot_general(a, b, (((1,), (1,)), ((), ())), preferred_element_type=F32)


def dot_tn(a, b):
    return lax.dot_general(a, b, (((0,), (0,)), ((), ())), preferred_element_type=F32)


def tiles(total, size=256):
    return [(start, min(size, total - start)) for start in range(0, total, size)]


def row_loop(total, step, fn):
    def it(i, carry):
        fn(pl.ds(pl.multiple_of(i * step, step), step))
        return carry

    lax.fori_loop(0, total // step, it, 0)


def kernel(cfg, names, *refs):
    NX, NW, T, D, LW, HW, HP = cfg
    r = types.SimpleNamespace(**dict(zip(names, refs, strict=True)))
    c = lax.axis_index("section")
    x = lax.axis_index("seq")
    w = lax.axis_index("wa")
    last = (x + 1) // NX
    first = (NX - x) // NX
    own = pl.ds(pl.multiple_of(w * ROWS, ROWS), ROWS)
    core_peer = (1 - c, x, w)
    NY = NZ = next(i for i in range(1, NW + 1) if i * i >= NW)
    z = w // NY
    y = w - z * NY
    LO, HI = pl.ds(0, D // 2), pl.ds(D // 2, D // 2)
    w_last = (w + 1) // NW
    w_first = (NW - w) // NW
    end = last * w_last
    begin = first * w_first
    next_dev = (c + end * (1 - 2 * c), lax.rem(x + w_last, NX), lax.rem(w + 1, NW))
    prev_dev = (c + begin * (1 - 2 * c), lax.rem(x + NX - w_first, NX), lax.rem(w + NW - 1, NW))

    def y_at(i):
        return lax.rem(y + i, NY)

    def z_at(i):
        return lax.rem(z + i, NZ)

    def y_peer(i):
        return (c, x, z * NY + y_at(i))

    def z_peer(i):
        return (c, x, z_at(i) * NY + y)

    def flat(ref, *cols):
        value = ref[(slice(None),) * 3 + cols] if cols else ref[...]
        return value.reshape(T, value.shape[-1])

    def wa_peer(i):
        return (c, x, lax.rem(w + i, NW))

    def x_peer(i):
        return (c, lax.rem(x + i, NX), w)

    def remote(src, dst, send, recv, dev):
        return pltpu.make_async_remote_copy(
            src_ref=src, dst_ref=dst, send_sem=send, recv_sem=recv, device_id=dev, device_id_type=MESH
        )

    def await_bytes(ref, sem):
        pltpu.make_async_copy(ref, ref, sem).wait()

    loads = []

    def load(src, dst):
        cp = pltpu.make_async_copy(src, dst, r.lsem.at[len(loads)])
        cp.start()
        loads.append(cp)
        return len(loads) - 1

    wpairs = [
        (r.w_in, r.Cown.at[c, pl.ds(0, 3)]),
        (r.w_small, r.Wsm.at[c]),
        (r.w_gu, r.Wgu.at[c, :, pl.ds(0, HW)]),
        (r.w_dn, r.Wdn.at[c, pl.ds(0, HW)]),
        (r.w_out, r.Cown.at[c, 3]),
    ]
    l_tok = [load(r.tokens.at[c], r.tok.at[0]), None]
    l_w = [load(*wpairs[0]), load(*wpairs[1])]
    l_tok[1] = load(r.tokens.at[2 + c], r.tok.at[1])
    l_w += [load(*p) for p in wpairs[2:]]
    l_cot = [load(r.cotangent.at[2 * k + c], r.cot.at[k]) for k in range(CHUNKS)]

    bar = pltpu.get_barrier_semaphore()

    def sig(dev):
        pl.semaphore_signal(bar, inc=1, device_id=dev, device_id_type=MESH)

    sig(core_peer)

    def sig_wa(i, carry):
        sig(wa_peer(i))
        return carry

    lax.fori_loop(1, NW, sig_wa, 0)
    for i in range(1, NX):
        sig(x_peer(i))
    sig((1 - c, lax.rem(x + 1, NX), w))
    sig((1 - c, lax.rem(x + NX - 1, NX), w))
    sig(next_dev)
    sig(prev_dev)
    if HP > HW:
        for l in range(2):
            r.Wdn[l, HW:] = jnp.zeros((HP - HW, D), BF)
            r.Wgu[l, :, HW:] = jnp.zeros((2, HP - HW, D), BF)
    r.gacc[...] = jnp.zeros(r.gacc.shape, F32)
    r.tacc[...] = jnp.zeros(r.tacc.shape, F32)
    pl.semaphore_wait(bar, (NW - 1) + (NX - 1) + 5)

    wcopies = []
    for i, (src, dst) in enumerate(wpairs):
        cp = remote(src, dst, r.wsend.at[i], r.wrecv.at[i], core_peer)
        cp.start()
        wcopies.append(cp)
    wready = set()

    def need_w(i):
        if i not in wready:
            wready.add(i)
            loads[l_w[i]].wait()
            wcopies[i].wait_recv()

    full = r.Cfull
    HALF = D // 2
    LQ = LW // NX
    xrows = pl.ds(pl.multiple_of(x * LQ, LQ), LQ)
    clanes = pl.ds(pl.multiple_of(c * HALF, HALF), HALF)
    la, lb = (pl.ds(pl.multiple_of(c * HALF + h, HALF // 2), HALF // 2) for h in (0, HALF // 2))
    first_a, first_b = full.at[:, 0, 0 : NY - 1, xrows, la], full.at[:, 0 : NZ - 1, 0, xrows, lb]
    second_a, second_b = full.at[:, 0 : NZ - 1, :, xrows, la], full.at[:, :, 0 : NY - 1, xrows, lb]

    def gather_wa():
        need_w(0)
        need_w(1)
        need_w(4)
        local = pltpu.make_async_copy(
            r.Cown.at[1, :, xrows, clanes], full.at[:, z, y, xrows, clanes], r.gwsem.at[0]
        )
        local.start()
        for lanes, peer, count, sem in ((la, y_peer, NY, 1), (lb, z_peer, NZ, 5)):
            for i in range(1, count):
                remote(
                    r.Cown.at[1, :, xrows, lanes], full.at[:, z, y, xrows, lanes],
                    r.gwsem.at[sem], r.gwsem.at[sem + 1], peer(i),
                ).start()
        tap = r.Wsm.at[1, :, pl.ds(0, 128)]
        tap_dst = r.taps1.at[w]
        tap_dst[...] = tap[...]

        def it(i, carry):
            remote(tap, tap_dst, r.gwsem.at[3], r.gwsem.at[4], wa_peer(i)).start()
            return carry

        lax.fori_loop(1, NW, it, 0)
        local.wait()

    def gather_mid():
        await_bytes(first_a, r.gwsem.at[2])
        piece = full.at[:, z, :, xrows, la]
        for i in range(1, NZ):
            remote(piece, piece, r.gwsem.at[7], r.gwsem.at[8], z_peer(i)).start()
        await_bytes(first_b, r.gwsem.at[6])
        piece = full.at[:, :, y, xrows, lb]
        for i in range(1, NY):
            remote(piece, piece, r.gwsem.at[9], r.gwsem.at[10], y_peer(i)).start()

    def gather_x(p):
        if p == 0:
            await_bytes(second_a, r.gwsem.at[8])
            await_bytes(second_b, r.gwsem.at[10])
        piece = full.at[p, :, :, xrows, clanes]
        for j in range(1, NX):
            remote(piece, piece, r.gxs.at[p], r.gxr.at[p], x_peer(j)).start()

    def gather_core(p):
        await_bytes(full.at[p, :, :, pl.ds(0, (NX - 1) * LQ), clanes], r.gxr.at[p])
        piece = full.at[p, :, :, :, clanes]
        remote(piece, piece, r.gcs.at[p], r.gcr.at[p], core_peer).start()

    def gather_done(p):
        await_bytes(full.at[p, :, :, :, clanes], r.gcr.at[p])

    def gather_close():
        for ref, sem in ((first_a, 1), (first_b, 5), (second_a, 7), (second_b, 9)):
            await_bytes(ref, r.gwsem.at[sem])
        await_bytes(r.taps1.at[pl.ds(0, NW - 1)], r.gwsem.at[3])
        for p in range(4):
            await_bytes(full.at[p, :, :, pl.ds(0, (NX - 1) * LQ), clanes], r.gxs.at[p])
            await_bytes(full.at[p, :, :, :, clanes], r.gcs.at[p])

    counts = {"ag": 0, "rs": 0}
    ag_sent, rs_sent = [], []

    def ag_start(buf):
        n = counts["ag"]
        counts["ag"] += 1
        lo, hi = buf.at[z, y, :, LO], buf.at[z, y, :, HI]
        for i in range(1, NY):
            remote(lo, lo, r.ags.at[n, 0], r.agr.at[n, 0], y_peer(i)).start()
            remote(hi, hi, r.ags.at[n, 1], r.agr.at[n, 1], z_peer(i)).start()
        ag_sent.append((n, buf))
        return n

    def ag_first(buf):
        return buf.at[0, pl.ds(0, NY - 1), :, LO]

    def ag_second(buf):
        return buf.at[pl.ds(0, NZ - 1), :, :, LO]

    def ag_mid(n, buf):
        lo, hi = buf.at[z, :, :, LO], buf.at[:, y, :, HI]
        await_bytes(ag_first(buf), r.agr.at[n, 0])
        for i in range(1, NZ):
            remote(lo, lo, r.ags.at[n, 2], r.agr.at[n, 2], z_peer(i)).start()
        await_bytes(ag_first(buf), r.agr.at[n, 1])
        for i in range(1, NY):
            remote(hi, hi, r.ags.at[n, 3], r.agr.at[n, 3], y_peer(i)).start()

    def ag_wait(n, buf):
        for i in (2, 3):
            await_bytes(ag_second(buf), r.agr.at[n, i])

    stage_use = [[], []]

    def stage_get(k):
        uses = stage_use[k]
        slot = len(uses) % 2
        if len(uses) >= 2:
            stage_sent(*uses[-2])
        return r.stage.at[k, slot]

    def stage_sent(n, buf):
        for i in (0, 1):
            await_bytes(ag_second(buf), r.rss.at[n, i])

    def rs_start(k, buf):
        n = counts["rs"]
        counts["rs"] += 1
        for i in range(1, NY):
            remote(
                buf.at[:, y_at(i), :, LO], r.rva.at[n, y], r.rss.at[n, 0], r.rsr.at[n, 0], y_peer(i)
            ).start()
            remote(
                buf.at[z_at(i), :, :, HI], r.rvb.at[n, z], r.rss.at[n, 1], r.rsr.at[n, 1], z_peer(i)
            ).start()
        stage_use[k].append((n, buf))
        return n

    def rs_mid(n, k):
        buf = dict(stage_use[k])[n]
        sa, sb = r.rsa.at[n], r.rsb.at[n]
        await_bytes(r.rva.at[n, pl.ds(0, NY - 1)], r.rsr.at[n, 0])
        total = buf[:, y, :, LO].astype(F32)
        for i in range(1, NY):
            total = total + r.rva[n, y_at(i)].astype(F32)
        sa[...] = total.astype(BF)
        for i in range(1, NZ):
            remote(sa.at[z_at(i)], r.rwa.at[n, z], r.rss.at[n, 2], r.rsr.at[n, 2], z_peer(i)).start()
        await_bytes(r.rvb.at[n, pl.ds(0, NZ - 1)], r.rsr.at[n, 1])
        total = buf[z, :, :, HI].astype(F32)
        for i in range(1, NZ):
            total = total + r.rvb[n, z_at(i)].astype(F32)
        sb[...] = total.astype(BF)
        for i in range(1, NY):
            remote(sb.at[y_at(i)], r.rwb.at[n, y], r.rss.at[n, 3], r.rsr.at[n, 3], y_peer(i)).start()

    def rs_sum(n):
        await_bytes(r.rwa.at[n, pl.ds(0, NZ - 1)], r.rsr.at[n, 2])
        lo = r.rsa[n, z].astype(F32)
        for i in range(1, NZ):
            lo = lo + r.rwa[n, z_at(i)].astype(F32)
        await_bytes(r.rwb.at[n, pl.ds(0, NY - 1)], r.rsr.at[n, 3])
        hi = r.rsb[n, y].astype(F32)
        for i in range(1, NY):
            hi = hi + r.rwb[n, y_at(i)].astype(F32)
        return jnp.concatenate([lo, hi], 1)

    def mids(kind, l, name, ks):
        for k in ks:
            if kind == "rs":
                rs_mid(rs_id[name, l, k], k)
            else:
                key, buf = {
                    "n": (("n", l, k), r.norm.at[l, k]),
                    "u": (("u", k), r.u1.at[k]),
                    "r": (("r", l, k), r.rb.at[l, k]),
                    "g": (("g", k), r.gbf.at[k]),
                }[name]
                ag_mid(ag_id[key], buf)

    rs_id, ag_id = {}, {}

    def u_of(l, k):
        return r.tok.at[k] if l == 0 else r.u1.at[k]

    hcopy = {}

    w0 = r.Cown.at[0]

    def put(ref, n0, n, value):
        ref[:, :, :, n0 : n0 + n] = value.astype(BF).reshape(NZ, NY, ROWS, n)

    def s1(l, k):
        u = u_of(l, k)
        loads[l_tok[k]].wait()
        need_w(0)
        projected = dot_nt(u[...], w0[0:3].reshape(3 * LW, D))
        b_part = projected[:, :LW]
        x_part = projected[:, 2 * LW :]
        r.projB[k] = b_part
        r.projC[k] = projected[:, LW : 2 * LW]
        r.projX[k] = x_part
        gated = (b_part * x_part).astype(BF)
        r.gp[k, pl.ds(8, T)] = gated.astype(F32)
        r.hs[k] = gated[T - 16 :]

        slot = k + last * c

        def send():
            remote(
                r.hs.at[k],
                r.hb.at[slot],
                r.hsend.at[k],
                r.hrecv.at[slot],
                (c + last * (1 - 2 * c), lax.rem(x + 1, NX), w),
            ).start()

        if k == CHUNKS - 1:
            pl.when(last * c == 0)(send)
        else:
            send()

    def s2(l, k):
        def get():
            await_bytes(r.hb.at[k], r.hrecv.at[k])

        def zero():
            r.hb[k] = jnp.zeros((16, LW), BF)

        if k == 0:
            none = first * (1 - c)
            pl.when(none == 0)(get)
            pl.when(none == 1)(zero)
        else:
            get()
        need_w(1)
        need_w(4)
        r.gp[k, pl.ds(0, 8)] = r.hb[k].astype(F32)[8:]
        taps = r.Wsm[l]
        conv = (
            taps[1:2, :LW] * r.gp[k, pl.ds(6, T)]
            + taps[2:3, :LW] * r.gp[k, pl.ds(7, T)]
            + taps[3:4, :LW] * r.gp[k, pl.ds(8, T)]
        )
        r.conv[k] = conv
        r.mixed[k] = (r.projC[k] * conv).astype(BF)
        buf = stage_get(k)
        for n0, n in tiles(D):
            put(buf, n0, n, dot_nn(r.mixed[k], w0[3, :, n0 : n0 + n]))
        rs_id["a", l, k] = rs_start(k, buf)

    def inv_rms(res):
        return lax.rsqrt(jnp.mean(res * res, -1, keepdims=True) + EPSILON)

    def s3(l, k):
        res = r.tok[k, own].astype(F32) + rs_sum(rs_id["a", l, k])
        r.res[l, k] = res
        buf = r.norm.at[l, k]
        buf[z, y] = (res * inv_rms(res) * r.Wsm[l, 0:1]).astype(BF)
        ag_id["n", l, k] = ag_start(buf)

    def s4(l, k):
        buf = r.norm.at[l, k]
        ag_wait(ag_id["n", l, k], buf)
        need_w(2)
        need_w(3)
        gu = r.gu.at[l, k]
        for g in range(2):
            gu[:, g * HP : (g + 1) * HP] = dot_nt(flat(buf), r.Wgu[l, g])

        def act(rows):
            gate = gu[rows, :HP]
            up = gu[rows, HP:]
            r.hid[l, k, rows] = (gate * jax.nn.sigmoid(gate) * up).astype(BF)

        row_loop(T, 32, act)
        st = stage_get(k)
        for n0, n in tiles(D):
            put(st, n0, n, dot_nn(r.hid[l, k], r.Wdn[l, :, n0 : n0 + n]))
        rs_id["b", l, k] = rs_start(k, st)

    def emit(l, k, value, staging, target, sems):
        staging[l, k] = value

        @pl.when(c == l)
        def _():
            target[2 * k + c] = value

        @pl.when(c != l)
        def _():
            remote(
                staging.at[l, k],
                target.at[2 * k + c],
                r.osend.at[sems, k],
                r.orecv.at[sems, k],
                core_peer,
            ).start()

    def s5(l, k):
        rows = (r.res[l, k] + rs_sum(rs_id["b", l, k])).astype(BF)
        if l == 0:
            r.u1[k, z, y] = rows
        emit(l, k, rows, r.lost, r.lo, 0)

    def outbf(l, k):
        return r.cotb.at[k] if l == 1 else r.gbf.at[k]

    def prep_cot(k):
        loads[l_cot[k]].wait()

        def cast(rows):
            r.cotb[k, rows] = r.cot[k, rows].astype(BF)

        row_loop(T, 32, cast)

    def t1(l, k):
        ob = outbf(l, k)
        if l == 0:
            ag_wait(ag_id["g", k], ob)
        hg = r.hg.at[k]
        for n0, n in tiles(HP):
            hg[:, n0 : n0 + n] = dot_nt(ob[...] if l == 1 else flat(ob), r.Wdn[l, n0 : n0 + n])
        gu = r.gu.at[l, k]
        gub = r.gub.at[l, k]

        def act(rows):
            gate = gu[rows, :HP]
            up = gu[rows, HP:]
            h = hg[rows]
            s = jax.nn.sigmoid(gate)
            gub[rows, :HP] = (h * up * (s * (1.0 + gate * (1.0 - s)))).astype(BF)
            gub[rows, HP:] = (h * (gate * s)).astype(BF)

        row_loop(T, 32, act)
        st = stage_get(k)
        for n0, n in tiles(D):
            put(st, n0, n, dot_nn(gub[...], r.Wgu[l, :, :, n0 : n0 + n].reshape(2 * HP, n)))
        rs_id["c", l, k] = rs_start(k, st)

    def t2(l, k):
        ng = rs_sum(rs_id["c", l, k])
        res = r.res[l, k]
        inv = inv_rms(res)
        g = r.cot[k, own] if l == 1 else r.g0own[k]
        r.gacc[l] = r.gacc[l] + jnp.sum(ng * res * inv, 0, keepdims=True)
        scaled = ng * r.Wsm[l, 0:1]
        rg = g + inv * scaled - res * (inv * inv * inv) * jnp.mean(scaled * res, -1, keepdims=True)
        r.rg[l, k] = rg
        buf = r.rb.at[l, k]
        buf[z, y] = rg.astype(BF)
        if l == 0:
            ag_id["r", l, k] = ag_start(buf)

    def t3(l, k):
        buf = r.rb.at[l, k]
        ag_wait(ag_id["r", l, k], buf)
        mg = dot_nt(flat(buf), w0[3])
        r.pbf[k, :, LW : 2 * LW] = (mg * r.conv[k]).astype(BF)
        cvg = mg * r.projC[k]
        r.cvg[k, pl.ds(0, T)] = cvg
        r.hgs[k] = cvg[:8]
        slot = k - first * (1 - c)

        def send():
            remote(
                r.hgs.at[k],
                r.hgb.at[slot],
                r.hgsend.at[k],
                r.hgrecv.at[slot],
                (c + first * (1 - 2 * c), lax.rem(x + NX - 1, NX), w),
            ).start()

        if k == 0:
            pl.when(first * (1 - c) == 0)(send)
        else:
            send()

    def t4(l, k):
        def get():
            await_bytes(r.hgb.at[k], r.hgrecv.at[k])

        def zero():
            r.hgb[k] = jnp.zeros((8, LW), F32)

        if k == CHUNKS - 1:
            none = last * c
            pl.when(none == 0)(get)
            pl.when(none == 1)(zero)
        else:
            get()
        e = r.cvg.at[k]
        e[pl.ds(T, 8)] = r.hgb[k]
        taps = r.Wsm[l]
        gg = (
            taps[3:4, :LW] * e[pl.ds(0, T)]
            + taps[2:3, :LW] * e[pl.ds(1, T)]
            + taps[1:2, :LW] * e[pl.ds(2, T)]
        )
        pbf = r.pbf.at[k]
        pbf[:, :LW] = (gg * r.projX[k]).astype(BF)
        pbf[:, 2 * LW :] = (gg * r.projB[k]).astype(BF)
        st = stage_get(k)
        for n0, n in tiles(D):
            put(st, n0, n, dot_nn(pbf[...], w0[0:3, :, n0 : n0 + n].reshape(3 * LW, n)))
        rs_id["d", l, k] = rs_start(k, st)
        cvg = e[pl.ds(0, T)]
        for j in range(3):
            r.tacc[j : j + 1, :LW] = r.tacc[j : j + 1, :LW] + jnp.sum(
                cvg * r.gp[k, pl.ds(6 + j, T)], 0, keepdims=True
            )

    def t5(l, k):
        rows = r.rg[l, k] + rs_sum(rs_id["d", l, k])
        emit(l, k, rows, r.ligst, r.ig, 1)

    def full_in():
        return full[0:3].reshape(3 * D, D)

    def taps_row(j):
        return jnp.concatenate([r.taps1[i, j : j + 1, :LW] for i in range(NW)], 1)

    def f1a():
        u = jnp.concatenate([r.u1[k, z, y] for k in range(CHUNKS)], 0)
        for p in range(3):
            gather_done(p)
            if p == 1:
                gather_core(2)
            r.proj1[p] = dot_nt(u, full[p].reshape(D, D))
        gated = (r.proj1[0] * r.proj1[2]).astype(BF)
        for k in range(CHUNKS):
            g = gated[k * ROWS : (k + 1) * ROWS]
            r.gp1[k, pl.ds(8, ROWS)] = g.astype(F32)
            r.h1s[k] = g
            slot = k + end * c

            def send(k=k, slot=slot):
                remote(
                    r.h1s.at[k], r.h1b.at[slot], r.h1send.at[k], r.h1recv.at[slot], next_dev
                ).start()

            if k == CHUNKS - 1:
                pl.when(end * c == 0)(send)
            else:
                send()

    def f1b():
        await_bytes(r.taps1.at[pl.ds(0, NW - 1)], r.gwsem.at[4])
        r.trow[...] = jnp.concatenate([taps_row(j + 1) for j in range(3)], 0)
        for k in range(CHUNKS):

            def get(k=k):
                await_bytes(r.h1b.at[k], r.h1recv.at[k])

            def zero(k=k):
                r.h1b[k] = jnp.zeros((ROWS, D), BF)

            if k == 0:
                none = begin * (1 - c)
                pl.when(none == 0)(get)
                pl.when(none == 1)(zero)
            else:
                get()
            r.gp1[k, pl.ds(0, 8)] = r.h1b[k].astype(F32)[8:]
            conv = sum(r.trow[j : j + 1] * r.gp1[k, pl.ds(6 + j, ROWS)] for j in range(3))
            r.conv1[k] = conv
            rows = slice(k * ROWS, (k + 1) * ROWS)
            r.mixed1[rows] = (r.proj1[1, rows] * conv).astype(BF)
        gather_done(3)
        wide = dot_nn(r.mixed1[...], full[3].reshape(D, D))
        for k in range(CHUNKS):
            res = r.u1[k, z, y].astype(F32) + wide[k * ROWS : (k + 1) * ROWS]
            r.res[1, k] = res
            buf = r.norm.at[1, k]
            buf[z, y] = (res * inv_rms(res) * r.Wsm[1, 0:1]).astype(BF)
            ag_id["n", 1, k] = ag_start(buf)

    def u_start():
        for k in range(CHUNKS):
            ag_id["u", k] = ag_start(r.u1.at[k])

    def b1a():
        rb = jnp.concatenate([r.rb[1, k, z, y] for k in range(CHUNKS)], 0)
        mg = dot_nt(rb, full[3].reshape(D, D))
        for k in range(CHUNKS):
            rows = slice(k * ROWS, (k + 1) * ROWS)
            m = mg[rows]
            cvg = m * r.proj1[1, rows]
            r.cv1[k, pl.ds(0, ROWS)] = cvg
            r.pbf1[rows, D : 2 * D] = (m * r.conv1[k]).astype(BF)
            slot = k - begin * (1 - c)

            def send(k=k, slot=slot):
                remote(
                    r.cv1.at[k, pl.ds(0, 8)], r.hg1b.at[slot], r.hg1send.at[k], r.hg1recv.at[slot], prev_dev
                ).start()

            if k == 0:
                pl.when(begin * (1 - c) == 0)(send)
            else:
                send()

    def b1b():
        taps = [0.0, 0.0, 0.0]
        for k in range(CHUNKS):

            def get(k=k):
                await_bytes(r.hg1b.at[k], r.hg1recv.at[k])

            def zero(k=k):
                r.hg1b[k] = jnp.zeros((8, D), F32)

            if k == CHUNKS - 1:
                none = end * c
                pl.when(none == 0)(get)
                pl.when(none == 1)(zero)
            else:
                get()
            e = r.cv1.at[k]
            e[pl.ds(ROWS, 8)] = r.hg1b[k]
            gg = sum(r.trow[2 - j : 3 - j] * e[pl.ds(j, ROWS)] for j in range(3))
            rows = slice(k * ROWS, (k + 1) * ROWS)
            r.pbf1[rows, :D] = (gg * r.proj1[2, rows]).astype(BF)
            r.pbf1[rows, 2 * D :] = (gg * r.proj1[0, rows]).astype(BF)
            cvg = e[pl.ds(0, ROWS)]
            for j in range(3):
                taps[j] = taps[j] + jnp.sum(cvg * r.gp1[k, pl.ds(6 + j, ROWS)], 0, keepdims=True)
        r.tap1g[...] = jnp.concatenate(taps, 0)
        wide = dot_nn(r.pbf1[...], full_in())
        for k in (1, 0):
            rows = r.rg[1, k] + wide[k * ROWS : (k + 1) * ROWS]
            r.g0own[k] = rows
            u = r.gbf.at[k]
            u[z, y] = rows.astype(BF)
            ag_id["g", k] = ag_start(u)
            emit(1, k, rows, r.ligst, r.ig, 1)

    def b1_exchange():
        for k in range(CHUNKS):
            ag_id["r", 1, k] = ag_start(r.rb.at[1, k])
        for i in range(NW):
            lanes = slice(i * LW, (i + 1) * LW)
            for p in range(3):
                r.pms[i, :, p * LW : (p + 1) * LW] = r.pbf1[:, p * D + i * LW : p * D + (i + 1) * LW]
            r.pms[i, :, 3 * LW :] = r.mixed1[:, lanes]
        mine = r.pm.at[w]
        mine[...] = r.pms[w]

        def it(i, carry):
            dev = wa_peer(i)
            remote(r.pms.at[dev[2]], mine, r.pmsem.at[0], r.pmsem.at[1], dev).start()
            return carry

        lax.fori_loop(1, NW, it, 0)

    X = [r.Xgu, r.Xdn, r.Xcv]
    Y = [r.Ygu, r.Ydn, r.Ycv]
    R = [r.Rgu, r.Rdn, r.Rcv]
    O = [r.o_gu, r.o_dn, r.o_cv]
    by_row = [True, False, True]

    def part(ref, i, q):
        if by_row[i]:
            size = ref.shape[0] // NX
            return ref.at[pl.ds(pl.multiple_of(q * size, size), size)]
        size = ref.shape[1] // NX
        return ref.at[:, pl.ds(pl.multiple_of(q * size, size), size)]

    def w1(l):
        for n0, n in tiles(D):
            cols = slice(n0, n0 + n)
            for g in range(2):
                r.Xgu[l, g * HW : (g + 1) * HW, cols] = sum(
                    dot_tn(r.gub[l, k, :, g * HP : (g + 1) * HP], flat(r.norm.at[l, k], cols))
                    for k in range(CHUNKS)
                )[:HW].astype(BF)
        for n0, n in tiles(D):
            r.Xdn[l, :, n0 : n0 + n] = sum(
                dot_tn(
                    r.hid[l, k],
                    outbf(l, k)[:, n0 : n0 + n] if l == 1 else flat(outbf(l, k), slice(n0, n0 + n)),
                )
                for k in range(CHUNKS)
            )[:HW].astype(BF)

    def w2_0():
        for n0, n in tiles(D):
            cols = slice(n0, n0 + n)
            r.Xcv[0, : 3 * LW, cols] = sum(
                dot_tn(r.pbf[k], r.tok[k, :, cols]) for k in range(CHUNKS)
            ).astype(BF)
            r.Xcv[0, 3 * LW :, cols] = sum(
                dot_tn(r.mixed[k], flat(r.rb.at[0, k], cols)) for k in range(CHUNKS)
            ).astype(BF)

    def w2_1():
        await_bytes(r.pm.at[pl.ds(0, NW - 1)], r.pmsem.at[1])
        for k in range(CHUNKS):
            ag_wait(ag_id["u", k], r.u1.at[k])
            ag_wait(ag_id["r", 1, k], r.rb.at[1, k])
        pm = [r.pm[:, k * ROWS : (k + 1) * ROWS].reshape(T, 4 * LW) for k in range(CHUNKS)]
        for n0, n in tiles(D):
            cols = slice(n0, n0 + n)
            r.Xcv[1, : 3 * LW, cols] = sum(
                dot_tn(pm[k][:, : 3 * LW], flat(r.u1.at[k], cols)) for k in range(CHUNKS)
            ).astype(BF)
            r.Xcv[1, 3 * LW :, cols] = sum(
                dot_tn(pm[k][:, 3 * LW :], flat(r.rb.at[1, k], cols)) for k in range(CHUNKS)
            ).astype(BF)

    def core_send(l, i):
        @pl.when(c != l)
        def _():
            remote(X[i].at[l], Y[i], r.csend.at[i], r.crecv.at[i], core_peer).start()

    def x_reduce(l, i):
        @pl.when(c == l)
        def _():
            await_bytes(Y[i], r.crecv.at[i])
            rows_total = Y[i].shape[0]

            def add(rows):
                X[i][l, rows] = (X[i][l, rows].astype(F32) + Y[i][rows].astype(F32)).astype(BF)

            row_loop(rows_total, 32, add)
            mine = R[i].at[x]
            for j in range(1, NX):
                dev = x_peer(j)
                remote(
                    part(X[i].at[l], i, dev[1]), mine, r.xsend.at[i], r.xrecv.at[i], dev
                ).start()

    def x_gather(l, i):
        @pl.when(c == l)
        def _():
            await_bytes(R[i].at[pl.ds(0, NX - 1)], r.xrecv.at[i])
            src = part(X[i].at[l], i, x)
            R[i][x] = src[...]
            dst = part(Y[i], i, x)
            rows_total = dst.shape[0]

            def add(rows):
                total = R[i][0, rows].astype(F32)
                for j in range(1, NX):
                    total = total + R[i][j, rows].astype(F32)
                dst[rows] = total.astype(BF)

            row_loop(rows_total, 16, add)
            for j in range(1, NX):
                remote(dst, dst, r.vsend.at[i], r.vrecv.at[i], x_peer(j)).start()

    def x_finish(l, i):
        @pl.when(c == l)
        def _():
            await_bytes(R[i].at[pl.ds(0, NX - 1)], r.vrecv.at[i])
            await_bytes(R[i].at[pl.ds(0, NX - 1)], r.xsend.at[i])
            await_bytes(R[i].at[pl.ds(0, NX - 1)], r.vsend.at[i])
            pltpu.make_async_copy(Y[i], O[i], r.lsem.at[len(loads) + i]).start()

        @pl.when(c != l)
        def _():
            await_bytes(Y[i], r.csend.at[i])

    GR = D // 128

    def gain_send(l):
        st = r.gst.at[l]
        for i in range(GR):
            st[0, i : i + 1] = r.gacc[l, :, i * 128 : (i + 1) * 128]
        gain = st[0, 0:GR]
        for i in range(NW):
            st[i, 0:GR] = gain
            st[i, GR:] = jnp.zeros((8, 128), F32)
            if l == 1:
                st[i, GR : GR + 3, :LW] = r.tap1g[:, i * LW : (i + 1) * LW]
        mine = r.gex.at[l, w]
        mine[...] = st[w]

        def it(i, carry):
            dev = wa_peer(i)
            remote(st.at[dev[2]], mine, r.gsend.at[l], r.grecv.at[l], dev).start()
            return carry

        lax.fori_loop(1, NW, it, 0)

    def gain_recv(l):
        await_bytes(r.gex.at[l, pl.ds(0, NW - 1)], r.grecv.at[l])
        total = r.gex[l, 0]
        for i in range(1, NW):
            total = total + r.gex[l, i]
        r.sm[l] = total

    def small_send(l):
        if l == 0:
            r.sm[0, GR:] = r.sm[0, GR:] + r.tacc[...]

        @pl.when(c != l)
        def _():
            remote(r.sm.at[l], r.smY, r.csend.at[3], r.crecv.at[3], core_peer).start()

    def small_x(l):
        @pl.when(c == l)
        def _():
            await_bytes(r.smY, r.crecv.at[3])
            mine = r.smR.at[x]
            mine[...] = r.sm[l] + r.smY[...]
            for j in range(1, NX):
                remote(mine, mine, r.xsend.at[3], r.xrecv.at[3], x_peer(j)).start()

    def small_finish(l):
        @pl.when(c == l)
        def _():
            await_bytes(r.smR.at[pl.ds(0, NX - 1)], r.xrecv.at[3])
            total = r.smR[0]
            for j in range(1, NX):
                total = total + r.smR[j]
            r.o_small[...] = total
            await_bytes(r.smR.at[pl.ds(0, NX - 1)], r.xsend.at[3])

        @pl.when(c != l)
        def _():
            await_bytes(r.smY, r.csend.at[3])

    A, B = 0, 1
    AB, BA = (0, 1), (1, 0)
    s1(0, A)
    s1(0, B)
    gather_wa()
    s2(0, A)
    s2(0, B)
    gather_mid()
    mids("rs", 0, "a", AB)
    gather_x(0)
    s3(0, A)
    s3(0, B)
    gather_x(1)
    mids("ag", 0, "n", AB)
    s4(0, A)
    s4(0, B)
    gather_x(2)
    prep_cot(A)
    mids("rs", 0, "b", AB)
    gather_core(0)
    gather_x(3)
    prep_cot(B)
    s5(0, A)
    s5(0, B)
    gather_core(1)
    f1a()
    gather_core(3)
    f1b()
    mids("ag", 1, "n", AB)
    u_start()
    s4(1, A)
    s4(1, B)
    t1(1, B)
    mids("rs", 1, "b", AB)
    t1(1, A)
    mids("ag", 1, "u", AB)
    mids("rs", 1, "c", BA)
    w1(1)
    t2(1, B)
    t2(1, A)
    b1a()
    core_send(1, 0)
    core_send(1, 1)
    b1b()
    s5(1, A)
    s5(1, B)
    mids("ag", 0, "g", BA)
    gain_send(1)
    b1_exchange()
    x_reduce(1, 0)
    x_reduce(1, 1)
    t1(0, B)
    t1(0, A)
    w1(0)
    core_send(0, 0)
    core_send(0, 1)
    mids("rs", 0, "c", BA)
    mids("ag", 1, "r", BA)
    gain_recv(1)
    small_send(1)
    t2(0, B)
    t2(0, A)
    x_reduce(0, 0)
    x_reduce(0, 1)
    mids("ag", 0, "r", BA)
    gain_send(0)
    w2_1()
    core_send(1, 2)
    t3(0, B)
    t3(0, A)
    x_gather(1, 0)
    x_gather(1, 1)
    t4(0, B)
    t4(0, A)
    w2_0()
    core_send(0, 2)
    mids("rs", 0, "d", BA)
    x_gather(0, 0)
    x_gather(0, 1)
    x_reduce(1, 2)
    small_x(1)
    gain_recv(0)
    small_send(0)
    x_reduce(0, 2)
    small_x(0)
    t5(0, B)
    t5(0, A)
    x_gather(1, 2)
    x_gather(0, 2)
    for l in (1, 0):
        for i in range(3):
            x_finish(l, i)
        small_finish(l)
    gather_close()
    await_bytes(r.pm.at[pl.ds(0, NW - 1)], r.pmsem.at[0])

    for sems, staging, target, out in ((0, r.lost, r.lo, r.o_layer), (1, r.ligst, r.ig, r.o_grad)):
        for k in range(CHUNKS):
            await_bytes(staging.at[0, k], r.orecv.at[sems, k])
            await_bytes(staging.at[0, k], r.osend.at[sems, k])
        out[...] = target[...]
    for n, buf in ag_sent:
        for i in range(2):
            await_bytes(ag_first(buf), r.ags.at[n, i])
            await_bytes(ag_second(buf), r.ags.at[n, 2 + i])
    for uses in stage_use:
        for n, buf in uses[-2:]:
            stage_sent(n, buf)
        for n, buf in uses:
            await_bytes(r.rwa.at[n, pl.ds(0, NZ - 1)], r.rss.at[n, 2])
            await_bytes(r.rwb.at[n, pl.ds(0, NY - 1)], r.rss.at[n, 3])
    for l in range(2):
        await_bytes(r.gex.at[l, pl.ds(0, NW - 1)], r.gsend.at[l])
    for fsem, fbuf, bsem, bbuf, no_next, no_prev in (
        (r.hsend, r.hs, r.hgsend, r.hgs, last * c, first * (1 - c)),
        (r.h1send, r.h1s, r.hg1send, r.hg1b, end * c, begin * (1 - c)),
    ):
        for k in range(CHUNKS):

            def fwd(k=k, fsem=fsem, fbuf=fbuf):
                await_bytes(fbuf.at[k], fsem.at[k])

            def bwd(k=k, bsem=bsem, bbuf=bbuf):
                await_bytes(bbuf.at[k], bsem.at[k])

            if k == CHUNKS - 1:
                pl.when(no_next == 0)(fwd)
            else:
                fwd()
            if k == 0:
                pl.when(no_prev == 0)(bwd)
            else:
                bwd()
    for cp in wcopies:
        cp.wait_send()
    for i in range(3):
        pltpu.make_async_copy(Y[i], O[i], r.lsem.at[len(loads) + i]).wait()


def body(NX, NW, tokens, cotangent, in_weight, conv_weight, out_weight, norm_gain, gate_up_weight, down_weight):
    micro, T, D = tokens.shape
    LW = conv_weight.shape[2]
    HW = gate_up_weight.shape[3]
    HP = -(-HW // 128) * 128
    w_small = jnp.concatenate(
        [norm_gain, jnp.pad(conv_weight[0], ((0, 4), (0, D - LW)))], 0
    )
    GR = D // 128
    L, K = 2, CHUNKS
    vmem = pltpu.VMEM
    dma = pltpu.SemaphoreType.DMA
    n_ag, n_rs = 6 * K, 6 * K
    NY = NZ = next(i for i in range(1, NW + 1) if i * i >= NW)
    plane = (NZ, NY, ROWS, D)
    ins = dict(
        tokens=tokens, cotangent=cotangent, w_in=in_weight[0].transpose(1, 2, 0), w_out=out_weight[0],
        w_gu=gate_up_weight[0].transpose(1, 2, 0), w_dn=down_weight[0], w_small=w_small
    )
    anyspec = pl.BlockSpec(memory_space=pl.ANY)
    vspec = pl.BlockSpec(memory_space=pltpu.VMEM)
    shape = jax.ShapeDtypeStruct
    outs = dict(
        o_layer=(shape((micro, ROWS, D), BF), vspec),
        o_grad=(shape((micro, ROWS, D), F32), vspec),
        o_cv=(shape((4 * LW, D), BF), anyspec),
        o_gu=(shape((2 * HW, D), BF), anyspec),
        o_dn=(shape((HW, D), BF), anyspec),
        o_small=(shape((GR + 8, 128), F32), vspec),
    )
    scratch = dict(
        Cown=vmem((L, 4, LW, D), BF), Cfull=vmem((4, NZ, NY, LW, D), BF),
        Wgu=vmem((L, 2, HP, D), BF), Wdn=vmem((L, HP, D), BF), Wsm=vmem((L, 8, D), F32),
        tok=vmem((K, T, D), BF), cot=vmem((K, T, D), F32), cotb=vmem((K, T, D), BF),
        projB=vmem((K, T, LW), F32), projC=vmem((K, T, LW), F32), projX=vmem((K, T, LW), F32),
        gp=vmem((K, T + 8, LW), F32), conv=vmem((K, T, LW), F32), mixed=vmem((K, T, LW), BF),
        gu=vmem((L, K, T, 2 * HP), F32), hg=vmem((K, T, HP), F32), hid=vmem((L, K, T, HP), BF),
        gub=vmem((L, K, T, 2 * HP), BF), pbf=vmem((K, T, 3 * LW), BF),
        res=vmem((L, K, ROWS, D), F32), rg=vmem((L, K, ROWS, D), F32), g0own=vmem((K, ROWS, D), F32),
        cvg=vmem((K, T + 8, LW), F32),
        norm=vmem((L, K) + plane, BF), u1=vmem((K,) + plane, BF), rb=vmem((L, K) + plane, BF), gbf=vmem((K,) + plane, BF),
        stage=vmem((K, 2) + plane, BF), rva=vmem((n_rs, NY, NZ, ROWS, D // 2), BF), rvb=vmem((n_rs, NZ, NY, ROWS, D // 2), BF),
        rsa=vmem((n_rs, NZ, ROWS, D // 2), BF), rsb=vmem((n_rs, NY, ROWS, D // 2), BF),
        rwa=vmem((n_rs, NZ, ROWS, D // 2), BF), rwb=vmem((n_rs, NY, ROWS, D // 2), BF),
        hs=vmem((K, 16, LW), BF), hb=vmem((K, 16, LW), BF), hgs=vmem((K, 8, LW), F32), hgb=vmem((K, 8, LW), F32),
        proj1=vmem((3, K * ROWS, D), F32), gp1=vmem((K, ROWS + 8, D), F32), conv1=vmem((K, ROWS, D), F32),
        mixed1=vmem((K * ROWS, D), BF), cv1=vmem((K, ROWS + 8, D), F32), pbf1=vmem((K * ROWS, 3 * D), BF),
        h1s=vmem((K, ROWS, D), BF), h1b=vmem((K, ROWS, D), BF), hg1b=vmem((K, 8, D), F32),
        trow=vmem((3, D), F32), tap1g=vmem((3, D), F32), taps1=vmem((NW, 8, 128), F32),
        pms=vmem((NW, K * ROWS, 4 * LW), BF), pm=vmem((NW, K * ROWS, 4 * LW), BF),
        lost=vmem((L, K, ROWS, D), BF), ligst=vmem((L, K, ROWS, D), F32),
        lo=vmem((micro, ROWS, D), BF), ig=vmem((micro, ROWS, D), F32),
        Xgu=vmem((L, 2 * HW, D), BF), Xdn=vmem((L, HW, D), BF), Xcv=vmem((L, 4 * LW, D), BF),
        Ygu=vmem((2 * HW, D), BF), Ydn=vmem((HW, D), BF), Ycv=vmem((4 * LW, D), BF),
        Rgu=vmem((NX, 2 * HW // NX, D), BF), Rdn=vmem((NX, HW, D // NX), BF), Rcv=vmem((NX, 4 * LW // NX, D), BF),
        gacc=vmem((L, 1, D), F32), tacc=vmem((8, 128), F32), gst=vmem((L, NW, GR + 8, 128), F32),
        gex=vmem((L, NW, GR + 8, 128), F32), sm=vmem((L, GR + 8, 128), F32),
        smY=vmem((GR + 8, 128), F32), smR=vmem((NX, GR + 8, 128), F32),
        lsem=dma((16,)), wsend=dma((5,)), wrecv=dma((5,)), ags=dma((n_ag, 4)), agr=dma((n_ag, 4)),
        rss=dma((n_rs, 4)), rsr=dma((n_rs, 4)), hsend=dma((K,)), hrecv=dma((K,)), hgsend=dma((K,)), hgrecv=dma((K,)),
        h1send=dma((K,)), h1recv=dma((K,)), hg1send=dma((K,)), hg1recv=dma((K,)), pmsem=dma((2,)),
        gwsem=dma((11,)), gxs=dma((4,)), gxr=dma((4,)), gcs=dma((4,)), gcr=dma((4,)),
        osend=dma((2, K)), orecv=dma((2, K)), csend=dma((4,)), crecv=dma((4,)), xsend=dma((4,)), xrecv=dma((4,)),
        vsend=dma((3,)), vrecv=dma((3,)), gsend=dma((L,)), grecv=dma((L,)),
    )
    names = tuple(ins) + tuple(outs) + tuple(scratch)
    layer, grad, g_cv, g_gu, g_dn, small = pl.pallas_call(
        functools.partial(kernel, (NX, NW, T, D, LW, HW, HP), names),
        out_shape=tuple(o[0] for o in outs.values()),
        in_specs=[anyspec] * len(ins),
        out_specs=tuple(o[1] for o in outs.values()),
        scratch_shapes=list(scratch.values()),
        compiler_params=pltpu.CompilerParams(
            collective_id=0, has_side_effects=True, vmem_limit_bytes=63 << 20
        ),
    )(*ins.values())
    return (
        layer[None],
        grad[None],
        g_cv[: 3 * LW].reshape(3, LW, D).transpose(2, 0, 1).astype(F32)[None],
        small[GR : GR + 3, :LW][None],
        g_cv[3 * LW :].astype(F32)[None],
        small[:GR].reshape(1, D),
        g_gu.reshape(2, HW, D).transpose(2, 0, 1).astype(F32)[None],
        g_dn.astype(F32)[None],
    )


def solution(mesh):
    in_specs = (
        P(None, "seq", None),
        P(None, "seq", None),
        P("section", None, None, "wa"),
        P("section", None, "wa"),
        P("section", "wa", None),
        P("section", None),
        P("section", None, None, "wa"),
        P("section", "wa", None),
    )
    out_specs = (
        P("section", None, ("seq", "wa"), None),
        P("section", None, ("seq", "wa"), None),
        P("section", None, None, "wa"),
        P("section", None, "wa"),
        P("section", "wa", None),
        P("section", None),
        P("section", None, None, "wa"),
        P("section", "wa", None),
    )
    fn = functools.partial(body, mesh.shape["seq"], mesh.shape["wa"])
    return jax.shard_map(fn, mesh=mesh, in_specs=in_specs, out_specs=out_specs, check_vma=False)
```

```python
import functools
import types

import jax
import jax.numpy as jnp
from jax import lax
from jax.experimental import pallas as pl
from jax.experimental.pallas import tpu as pltpu
from jax.sharding import PartitionSpec as P

EPSILON = 1e-05
MESH = pl.DeviceIdType.MESH
BF = jnp.bfloat16
F32 = jnp.float32
ROWS = 16
CHUNKS = 2


def dot_nn(a, b):
    return jnp.dot(a, b, preferred_element_type=F32)


def dot_nt(a, b):
    return lax.dot_general(a, b, (((1,), (1,)), ((), ())), preferred_element_type=F32)


def dot_tn(a, b):
    return lax.dot_general(a, b, (((0,), (0,)), ((), ())), preferred_element_type=F32)


def tiles(total, size=256):
    return [(start, min(size, total - start)) for start in range(0, total, size)]


def row_loop(total, step, fn):
    def it(i, carry):
        fn(pl.ds(pl.multiple_of(i * step, step), step))
        return carry

    lax.fori_loop(0, total // step, it, 0)


def kernel(cfg, names, *refs):
    NX, NW, T, D, LW, HW, HP = cfg
    r = types.SimpleNamespace(**dict(zip(names, refs, strict=True)))
    c = lax.axis_index("section")
    x = lax.axis_index("seq")
    w = lax.axis_index("wa")
    last = (x + 1) // NX
    first = (NX - x) // NX
    own = pl.ds(pl.multiple_of(w * ROWS, ROWS), ROWS)
    core_peer = (1 - c, x, w)
    NY = NZ = next(i for i in range(1, NW + 1) if i * i >= NW)
    z = w // NY
    y = w - z * NY
    LO, HI = pl.ds(0, D // 2), pl.ds(D // 2, D // 2)
    w_last = (w + 1) // NW
    w_first = (NW - w) // NW
    end = last * w_last
    begin = first * w_first
    next_dev = (c + end * (1 - 2 * c), lax.rem(x + w_last, NX), lax.rem(w + 1, NW))
    prev_dev = (c + begin * (1 - 2 * c), lax.rem(x + NX - w_first, NX), lax.rem(w + NW - 1, NW))

    def y_at(i):
        return lax.rem(y + i, NY)

    def z_at(i):
        return lax.rem(z + i, NZ)

    def y_peer(i):
        return (c, x, z * NY + y_at(i))

    def z_peer(i):
        return (c, x, z_at(i) * NY + y)

    def flat(ref, *cols):
        value = ref[(slice(None),) * 3 + cols] if cols else ref[...]
        return value.reshape(T, value.shape[-1])

    def wa_peer(i):
        return (c, x, lax.rem(w + i, NW))

    def x_peer(i):
        return (c, lax.rem(x + i, NX), w)

    def remote(src, dst, send, recv, dev):
        return pltpu.make_async_remote_copy(
            src_ref=src, dst_ref=dst, send_sem=send, recv_sem=recv, device_id=dev, device_id_type=MESH
        )

    def await_bytes(ref, sem):
        pltpu.make_async_copy(ref, ref, sem).wait()

    loads = []

    def load(src, dst):
        cp = pltpu.make_async_copy(src, dst, r.lsem.at[len(loads)])
        cp.start()
        loads.append(cp)
        return len(loads) - 1

    wpairs = [
        (r.w_in, r.Cown.at[c, pl.ds(0, 3)]),
        (r.w_small, r.Wsm.at[c]),
        (r.w_gu, r.Wgu.at[c, :, pl.ds(0, HW)]),
        (r.w_dn, r.Wdn.at[c, pl.ds(0, HW)]),
        (r.w_out, r.Cown.at[c, 3]),
    ]
    l_tok = [load(r.tokens.at[c], r.tok.at[0]), None]
    l_w = [load(*wpairs[0]), load(*wpairs[1])]
    l_tok[1] = load(r.tokens.at[2 + c], r.tok.at[1])
    l_w += [load(*p) for p in wpairs[2:]]
    l_cot = [load(r.cotangent.at[2 * k + c], r.cot.at[k]) for k in range(CHUNKS)]

    bar = pltpu.get_barrier_semaphore()

    def sig(dev):
        pl.semaphore_signal(bar, inc=1, device_id=dev, device_id_type=MESH)

    sig(core_peer)

    def sig_wa(i, carry):
        sig(wa_peer(i))
        return carry

    lax.fori_loop(1, NW, sig_wa, 0)
    for i in range(1, NX):
        sig(x_peer(i))
    sig((1 - c, lax.rem(x + 1, NX), w))
    sig((1 - c, lax.rem(x + NX - 1, NX), w))
    sig(next_dev)
    sig(prev_dev)
    if HP > HW:
        for l in range(2):
            r.Wdn[l, HW:] = jnp.zeros((HP - HW, D), BF)
            r.Wgu[l, :, HW:] = jnp.zeros((2, HP - HW, D), BF)
    r.gacc[...] = jnp.zeros(r.gacc.shape, F32)
    r.tacc[...] = jnp.zeros(r.tacc.shape, F32)
    pl.semaphore_wait(bar, (NW - 1) + (NX - 1) + 5)

    wcopies = []
    for i, (src, dst) in enumerate(wpairs):
        cp = remote(src, dst, r.wsend.at[i], r.wrecv.at[i], core_peer)
        cp.start()
        wcopies.append(cp)
    wready = set()

    def need_w(i):
        if i not in wready:
            wready.add(i)
            loads[l_w[i]].wait()
            wcopies[i].wait_recv()

    full = r.Cfull
    HALF = D // 2
    LQ = LW // NX
    xrows = pl.ds(pl.multiple_of(x * LQ, LQ), LQ)
    clanes = pl.ds(pl.multiple_of(c * HALF, HALF), HALF)
    la, lb = (pl.ds(pl.multiple_of(c * HALF + h, HALF // 2), HALF // 2) for h in (0, HALF // 2))
    first_a, first_b = full.at[:, 0, 0 : NY - 1, xrows, la], full.at[:, 0 : NZ - 1, 0, xrows, lb]
    second_a, second_b = full.at[:, 0 : NZ - 1, :, xrows, la], full.at[:, :, 0 : NY - 1, xrows, lb]

    def gather_wa():
        need_w(0)
        need_w(1)
        need_w(4)
        local = pltpu.make_async_copy(
            r.Cown.at[1, :, xrows, clanes], full.at[:, z, y, xrows, clanes], r.gwsem.at[0]
        )
        local.start()
        for lanes, peer, count, sem in ((la, y_peer, NY, 1), (lb, z_peer, NZ, 5)):
            for i in range(1, count):
                remote(
                    r.Cown.at[1, :, xrows, lanes], full.at[:, z, y, xrows, lanes],
                    r.gwsem.at[sem], r.gwsem.at[sem + 1], peer(i),
                ).start()
        tap = r.Wsm.at[1, :, pl.ds(0, 128)]
        tap_dst = r.taps1.at[w]
        tap_dst[...] = tap[...]

        def it(i, carry):
            remote(tap, tap_dst, r.gwsem.at[3], r.gwsem.at[4], wa_peer(i)).start()
            return carry

        lax.fori_loop(1, NW, it, 0)
        local.wait()

    def gather_mid():
        await_bytes(first_a, r.gwsem.at[2])
        piece = full.at[:, z, :, xrows, la]
        for i in range(1, NZ):
            remote(piece, piece, r.gwsem.at[7], r.gwsem.at[8], z_peer(i)).start()
        await_bytes(first_b, r.gwsem.at[6])
        piece = full.at[:, :, y, xrows, lb]
        for i in range(1, NY):
            remote(piece, piece, r.gwsem.at[9], r.gwsem.at[10], y_peer(i)).start()

    def gather_x(p):
        if p == 0:
            await_bytes(second_a, r.gwsem.at[8])
            await_bytes(second_b, r.gwsem.at[10])
        piece = full.at[p, :, :, xrows, clanes]
        for j in range(1, NX):
            remote(piece, piece, r.gxs.at[p], r.gxr.at[p], x_peer(j)).start()

    def gather_core(p):
        await_bytes(full.at[p, :, :, pl.ds(0, (NX - 1) * LQ), clanes], r.gxr.at[p])
        piece = full.at[p, :, :, :, clanes]
        remote(piece, piece, r.gcs.at[p], r.gcr.at[p], core_peer).start()

    def gather_done(p):
        await_bytes(full.at[p, :, :, :, clanes], r.gcr.at[p])

    def gather_close():
        for ref, sem in ((first_a, 1), (first_b, 5), (second_a, 7), (second_b, 9)):
            await_bytes(ref, r.gwsem.at[sem])
        await_bytes(r.taps1.at[pl.ds(0, NW - 1)], r.gwsem.at[3])
        for p in range(4):
            await_bytes(full.at[p, :, :, pl.ds(0, (NX - 1) * LQ), clanes], r.gxs.at[p])
            await_bytes(full.at[p, :, :, :, clanes], r.gcs.at[p])

    counts = {"ag": 0, "rs": 0}
    ag_sent, rs_sent = [], []

    def ag_start(buf):
        n = counts["ag"]
        counts["ag"] += 1
        lo, hi = buf.at[z, y, :, LO], buf.at[z, y, :, HI]
        for i in range(1, NY):
            remote(lo, lo, r.ags.at[n, 0], r.agr.at[n, 0], y_peer(i)).start()
            remote(hi, hi, r.ags.at[n, 1], r.agr.at[n, 1], z_peer(i)).start()
        ag_sent.append((n, buf))
        return n

    def ag_first(buf):
        return buf.at[0, pl.ds(0, NY - 1), :, LO]

    def ag_second(buf):
        return buf.at[pl.ds(0, NZ - 1), :, :, LO]

    def ag_mid(n, buf):
        lo, hi = buf.at[z, :, :, LO], buf.at[:, y, :, HI]
        await_bytes(ag_first(buf), r.agr.at[n, 0])
        for i in range(1, NZ):
            remote(lo, lo, r.ags.at[n, 2], r.agr.at[n, 2], z_peer(i)).start()
        await_bytes(ag_first(buf), r.agr.at[n, 1])
        for i in range(1, NY):
            remote(hi, hi, r.ags.at[n, 3], r.agr.at[n, 3], y_peer(i)).start()

    def ag_wait(n, buf):
        for i in (2, 3):
            await_bytes(ag_second(buf), r.agr.at[n, i])

    stage_use = [[], []]

    def stage_get(k):
        uses = stage_use[k]
        slot = len(uses) % 2
        if len(uses) >= 2:
            stage_sent(*uses[-2])
        return r.stage.at[k, slot]

    def stage_sent(n, buf):
        for i in (0, 1):
            await_bytes(ag_second(buf), r.rss.at[n, i])

    def rs_start(k, buf):
        n = counts["rs"]
        counts["rs"] += 1
        for i in range(1, NY):
            remote(
                buf.at[:, y_at(i), :, LO], r.rva.at[n, y], r.rss.at[n, 0], r.rsr.at[n, 0], y_peer(i)
            ).start()
            remote(
                buf.at[z_at(i), :, :, HI], r.rvb.at[n, z], r.rss.at[n, 1], r.rsr.at[n, 1], z_peer(i)
            ).start()
        stage_use[k].append((n, buf))
        return n

    def rs_mid(n, k):
        buf = dict(stage_use[k])[n]
        sa, sb = r.rsa.at[n], r.rsb.at[n]
        await_bytes(r.rva.at[n, pl.ds(0, NY - 1)], r.rsr.at[n, 0])
        total = buf[:, y, :, LO].astype(F32)
        for i in range(1, NY):
            total = total + r.rva[n, y_at(i)].astype(F32)
        sa[...] = total.astype(BF)
        for i in range(1, NZ):
            remote(sa.at[z_at(i)], r.rwa.at[n, z], r.rss.at[n, 2], r.rsr.at[n, 2], z_peer(i)).start()
        await_bytes(r.rvb.at[n, pl.ds(0, NZ - 1)], r.rsr.at[n, 1])
        total = buf[z, :, :, HI].astype(F32)
        for i in range(1, NZ):
            total = total + r.rvb[n, z_at(i)].astype(F32)
        sb[...] = total.astype(BF)
        for i in range(1, NY):
            remote(sb.at[y_at(i)], r.rwb.at[n, y], r.rss.at[n, 3], r.rsr.at[n, 3], y_peer(i)).start()

    def rs_sum(n):
        await_bytes(r.rwa.at[n, pl.ds(0, NZ - 1)], r.rsr.at[n, 2])
        lo = r.rsa[n, z].astype(F32)
        for i in range(1, NZ):
            lo = lo + r.rwa[n, z_at(i)].astype(F32)
        await_bytes(r.rwb.at[n, pl.ds(0, NY - 1)], r.rsr.at[n, 3])
        hi = r.rsb[n, y].astype(F32)
        for i in range(1, NY):
            hi = hi + r.rwb[n, y_at(i)].astype(F32)
        return jnp.concatenate([lo, hi], 1)

    def mids(kind, l, name, ks):
        for k in ks:
            if kind == "rs":
                rs_mid(rs_id[name, l, k], k)
            else:
                key, buf = {
                    "n": (("n", l, k), r.norm.at[l, k]),
                    "u": (("u", k), r.u1.at[k]),
                    "r": (("r", l, k), r.rb.at[l, k]),
                    "g": (("g", k), r.gbf.at[k]),
                }[name]
                ag_mid(ag_id[key], buf)

    rs_id, ag_id = {}, {}

    def u_of(l, k):
        return r.tok.at[k] if l == 0 else r.u1.at[k]

    hcopy = {}

    w0 = r.Cown.at[0]

    def put(ref, n0, n, value):
        ref[:, :, :, n0 : n0 + n] = value.astype(BF).reshape(NZ, NY, ROWS, n)

    def s1(l, k):
        u = u_of(l, k)
        loads[l_tok[k]].wait()
        need_w(0)
        projected = dot_nt(u[...], w0[0:3].reshape(3 * LW, D))
        b_part = projected[:, :LW]
        x_part = projected[:, 2 * LW :]
        r.projB[k] = b_part
        r.projC[k] = projected[:, LW : 2 * LW]
        r.projX[k] = x_part
        gated = (b_part * x_part).astype(BF)
        r.gp[k, pl.ds(8, T)] = gated.astype(F32)
        r.hs[k] = gated[T - 16 :]

        slot = k + last * c

        def send():
            remote(
                r.hs.at[k],
                r.hb.at[slot],
                r.hsend.at[k],
                r.hrecv.at[slot],
                (c + last * (1 - 2 * c), lax.rem(x + 1, NX), w),
            ).start()

        if k == CHUNKS - 1:
            pl.when(last * c == 0)(send)
        else:
            send()

    def s2(l, k):
        def get():
            await_bytes(r.hb.at[k], r.hrecv.at[k])

        def zero():
            r.hb[k] = jnp.zeros((16, LW), BF)

        if k == 0:
            none = first * (1 - c)
            pl.when(none == 0)(get)
            pl.when(none == 1)(zero)
        else:
            get()
        need_w(1)
        need_w(4)
        r.gp[k, pl.ds(0, 8)] = r.hb[k].astype(F32)[8:]
        taps = r.Wsm[l]
        conv = (
            taps[1:2, :LW] * r.gp[k, pl.ds(6, T)]
            + taps[2:3, :LW] * r.gp[k, pl.ds(7, T)]
            + taps[3:4, :LW] * r.gp[k, pl.ds(8, T)]
        )
        r.conv[k] = conv
        r.mixed[k] = (r.projC[k] * conv).astype(BF)
        buf = stage_get(k)
        for n0, n in tiles(D):
            put(buf, n0, n, dot_nn(r.mixed[k], w0[3, :, n0 : n0 + n]))
        rs_id["a", l, k] = rs_start(k, buf)

    def inv_rms(res):
        return lax.rsqrt(jnp.mean(res * res, -1, keepdims=True) + EPSILON)

    def s3(l, k):
        res = r.tok[k, own].astype(F32) + rs_sum(rs_id["a", l, k])
        r.res[l, k] = res
        buf = r.norm.at[l, k]
        buf[z, y] = (res * inv_rms(res) * r.Wsm[l, 0:1]).astype(BF)
        ag_id["n", l, k] = ag_start(buf)

    def s4(l, k):
        buf = r.norm.at[l, k]
        ag_wait(ag_id["n", l, k], buf)
        need_w(2)
        need_w(3)
        gu = r.gu.at[l, k]
        for g in range(2):
            gu[:, g * HP : (g + 1) * HP] = dot_nt(flat(buf), r.Wgu[l, g])

        def act(rows):
            gate = gu[rows, :HP]
            up = gu[rows, HP:]
            r.hid[l, k, rows] = (gate * jax.nn.sigmoid(gate) * up).astype(BF)

        row_loop(T, 32, act)
        st = stage_get(k)
        for n0, n in tiles(D):
            put(st, n0, n, dot_nn(r.hid[l, k], r.Wdn[l, :, n0 : n0 + n]))
        rs_id["b", l, k] = rs_start(k, st)

    def emit(l, k, value, staging, target, sems):
        staging[l, k] = value

        @pl.when(c == l)
        def _():
            target[2 * k + c] = value

        @pl.when(c != l)
        def _():
            remote(
                staging.at[l, k],
                target.at[2 * k + c],
                r.osend.at[sems, k],
                r.orecv.at[sems, k],
                core_peer,
            ).start()

    def s5(l, k):
        rows = (r.res[l, k] + rs_sum(rs_id["b", l, k])).astype(BF)
        if l == 0:
            r.u1[k, z, y] = rows
        emit(l, k, rows, r.lost, r.lo, 0)

    def outbf(l, k):
        return r.cotb.at[k] if l == 1 else r.gbf.at[k]

    def prep_cot(k):
        loads[l_cot[k]].wait()

        def cast(rows):
            r.cotb[k, rows] = r.cot[k, rows].astype(BF)

        row_loop(T, 32, cast)

    def t1(l, k):
        ob = outbf(l, k)
        if l == 0:
            ag_wait(ag_id["g", k], ob)
        hg = r.hg.at[k]
        for n0, n in tiles(HP):
            hg[:, n0 : n0 + n] = dot_nt(ob[...] if l == 1 else flat(ob), r.Wdn[l, n0 : n0 + n])
        gu = r.gu.at[l, k]
        gub = r.gub.at[l, k]

        def act(rows):
            gate = gu[rows, :HP]
            up = gu[rows, HP:]
            h = hg[rows]
            s = jax.nn.sigmoid(gate)
            gub[rows, :HP] = (h * up * (s * (1.0 + gate * (1.0 - s)))).astype(BF)
            gub[rows, HP:] = (h * (gate * s)).astype(BF)

        row_loop(T, 32, act)
        st = stage_get(k)
        for n0, n in tiles(D):
            put(st, n0, n, dot_nn(gub[...], r.Wgu[l, :, :, n0 : n0 + n].reshape(2 * HP, n)))
        rs_id["c", l, k] = rs_start(k, st)

    def t2(l, k):
        ng = rs_sum(rs_id["c", l, k])
        res = r.res[l, k]
        inv = inv_rms(res)
        g = r.cot[k, own] if l == 1 else r.g0own[k]
        r.gacc[l] = r.gacc[l] + jnp.sum(ng * res * inv, 0, keepdims=True)
        scaled = ng * r.Wsm[l, 0:1]
        rg = g + inv * scaled - res * (inv * inv * inv) * jnp.mean(scaled * res, -1, keepdims=True)
        r.rg[l, k] = rg
        buf = r.rb.at[l, k]
        buf[z, y] = rg.astype(BF)
        if l == 0:
            ag_id["r", l, k] = ag_start(buf)

    def t3(l, k):
        buf = r.rb.at[l, k]
        ag_wait(ag_id["r", l, k], buf)
        mg = dot_nt(flat(buf), w0[3])
        r.pbf[k, :, LW : 2 * LW] = (mg * r.conv[k]).astype(BF)
        cvg = mg * r.projC[k]
        r.cvg[k, pl.ds(0, T)] = cvg
        r.hgs[k] = cvg[:8]
        slot = k - first * (1 - c)

        def send():
            remote(
                r.hgs.at[k],
                r.hgb.at[slot],
                r.hgsend.at[k],
                r.hgrecv.at[slot],
                (c + first * (1 - 2 * c), lax.rem(x + NX - 1, NX), w),
            ).start()

        if k == 0:
            pl.when(first * (1 - c) == 0)(send)
        else:
            send()

    def t4(l, k):
        def get():
            await_bytes(r.hgb.at[k], r.hgrecv.at[k])

        def zero():
            r.hgb[k] = jnp.zeros((8, LW), F32)

        if k == CHUNKS - 1:
            none = last * c
            pl.when(none == 0)(get)
            pl.when(none == 1)(zero)
        else:
            get()
        e = r.cvg.at[k]
        e[pl.ds(T, 8)] = r.hgb[k]
        taps = r.Wsm[l]
        gg = (
            taps[3:4, :LW] * e[pl.ds(0, T)]
            + taps[2:3, :LW] * e[pl.ds(1, T)]
            + taps[1:2, :LW] * e[pl.ds(2, T)]
        )
        pbf = r.pbf.at[k]
        pbf[:, :LW] = (gg * r.projX[k]).astype(BF)
        pbf[:, 2 * LW :] = (gg * r.projB[k]).astype(BF)
        st = stage_get(k)
        for n0, n in tiles(D):
            put(st, n0, n, dot_nn(pbf[...], w0[0:3, :, n0 : n0 + n].reshape(3 * LW, n)))
        rs_id["d", l, k] = rs_start(k, st)
        cvg = e[pl.ds(0, T)]
        for j in range(3):
            r.tacc[j : j + 1, :LW] = r.tacc[j : j + 1, :LW] + jnp.sum(
                cvg * r.gp[k, pl.ds(6 + j, T)], 0, keepdims=True
            )

    def t5(l, k):
        rows = r.rg[l, k] + rs_sum(rs_id["d", l, k])
        emit(l, k, rows, r.ligst, r.ig, 1)

    def full_in():
        return full[0:3].reshape(3 * D, D)

    def taps_row(j):
        return jnp.concatenate([r.taps1[i, j : j + 1, :LW] for i in range(NW)], 1)

    def f1a():
        u = jnp.concatenate([r.u1[k, z, y] for k in range(CHUNKS)], 0)
        for p in range(3):
            gather_done(p)
            if p == 1:
                gather_core(2)
            r.proj1[p] = dot_nt(u, full[p].reshape(D, D))
        gated = (r.proj1[0] * r.proj1[2]).astype(BF)
        for k in range(CHUNKS):
            g = gated[k * ROWS : (k + 1) * ROWS]
            r.gp1[k, pl.ds(8, ROWS)] = g.astype(F32)
            r.h1s[k] = g
            slot = k + end * c

            def send(k=k, slot=slot):
                remote(
                    r.h1s.at[k], r.h1b.at[slot], r.h1send.at[k], r.h1recv.at[slot], next_dev
                ).start()

            if k == CHUNKS - 1:
                pl.when(end * c == 0)(send)
            else:
                send()

    def f1b():
        await_bytes(r.taps1.at[pl.ds(0, NW - 1)], r.gwsem.at[4])
        r.trow[...] = jnp.concatenate([taps_row(j + 1) for j in range(3)], 0)
        for k in range(CHUNKS):

            def get(k=k):
                await_bytes(r.h1b.at[k], r.h1recv.at[k])

            def zero(k=k):
                r.h1b[k] = jnp.zeros((ROWS, D), BF)

            if k == 0:
                none = begin * (1 - c)
                pl.when(none == 0)(get)
                pl.when(none == 1)(zero)
            else:
                get()
            r.gp1[k, pl.ds(0, 8)] = r.h1b[k].astype(F32)[8:]
            conv = sum(r.trow[j : j + 1] * r.gp1[k, pl.ds(6 + j, ROWS)] for j in range(3))
            r.conv1[k] = conv
            rows = slice(k * ROWS, (k + 1) * ROWS)
            r.mixed1[rows] = (r.proj1[1, rows] * conv).astype(BF)
        gather_done(3)
        wide = dot_nn(r.mixed1[...], full[3].reshape(D, D))
        for k in range(CHUNKS):
            res = r.u1[k, z, y].astype(F32) + wide[k * ROWS : (k + 1) * ROWS]
            r.res[1, k] = res
            buf = r.norm.at[1, k]
            buf[z, y] = (res * inv_rms(res) * r.Wsm[1, 0:1]).astype(BF)
            ag_id["n", 1, k] = ag_start(buf)

    def u_start():
        for k in range(CHUNKS):
            ag_id["u", k] = ag_start(r.u1.at[k])

    def b1a():
        rb = jnp.concatenate([r.rb[1, k, z, y] for k in range(CHUNKS)], 0)
        mg = dot_nt(rb, full[3].reshape(D, D))
        for k in range(CHUNKS):
            rows = slice(k * ROWS, (k + 1) * ROWS)
            m = mg[rows]
            cvg = m * r.proj1[1, rows]
            r.cv1[k, pl.ds(0, ROWS)] = cvg
            r.pbf1[rows, D : 2 * D] = (m * r.conv1[k]).astype(BF)
            slot = k - begin * (1 - c)

            def send(k=k, slot=slot):
                remote(
                    r.cv1.at[k, pl.ds(0, 8)], r.hg1b.at[slot], r.hg1send.at[k], r.hg1recv.at[slot], prev_dev
                ).start()

            if k == 0:
                pl.when(begin * (1 - c) == 0)(send)
            else:
                send()

    def b1b():
        taps = [0.0, 0.0, 0.0]
        for k in range(CHUNKS):

            def get(k=k):
                await_bytes(r.hg1b.at[k], r.hg1recv.at[k])

            def zero(k=k):
                r.hg1b[k] = jnp.zeros((8, D), F32)

            if k == CHUNKS - 1:
                none = end * c
                pl.when(none == 0)(get)
                pl.when(none == 1)(zero)
            else:
                get()
            e = r.cv1.at[k]
            e[pl.ds(ROWS, 8)] = r.hg1b[k]
            gg = sum(r.trow[2 - j : 3 - j] * e[pl.ds(j, ROWS)] for j in range(3))
            rows = slice(k * ROWS, (k + 1) * ROWS)
            r.pbf1[rows, :D] = (gg * r.proj1[2, rows]).astype(BF)
            r.pbf1[rows, 2 * D :] = (gg * r.proj1[0, rows]).astype(BF)
            cvg = e[pl.ds(0, ROWS)]
            for j in range(3):
                taps[j] = taps[j] + jnp.sum(cvg * r.gp1[k, pl.ds(6 + j, ROWS)], 0, keepdims=True)
        r.tap1g[...] = jnp.concatenate(taps, 0)
        wide = dot_nn(r.pbf1[...], full_in())
        for k in (1, 0):
            rows = r.rg[1, k] + wide[k * ROWS : (k + 1) * ROWS]
            r.g0own[k] = rows
            u = r.gbf.at[k]
            u[z, y] = rows.astype(BF)
            ag_id["g", k] = ag_start(u)
            emit(1, k, rows, r.ligst, r.ig, 1)

    def b1_exchange():
        for k in range(CHUNKS):
            ag_id["r", 1, k] = ag_start(r.rb.at[1, k])
        for i in range(NW):
            lanes = slice(i * LW, (i + 1) * LW)
            for p in range(3):
                r.pms[i, :, p * LW : (p + 1) * LW] = r.pbf1[:, p * D + i * LW : p * D + (i + 1) * LW]
            r.pms[i, :, 3 * LW :] = r.mixed1[:, lanes]
        mine = r.pm.at[w]
        mine[...] = r.pms[w]

        def it(i, carry):
            dev = wa_peer(i)
            remote(r.pms.at[dev[2]], mine, r.pmsem.at[0], r.pmsem.at[1], dev).start()
            return carry

        lax.fori_loop(1, NW, it, 0)

    X = [r.Xgu, r.Xdn, r.Xcv]
    Y = [r.Ygu, r.Ydn, r.Ycv]
    R = [r.Rgu, r.Rdn, r.Rcv]
    flush = [
        [(r.Ygu, r.o_gu)],
        [(r.Ydn, r.o_dn)],
        [(r.Ycv.at[pl.ds(0, 3 * LW)], r.o_in), (r.Ycv.at[pl.ds(3 * LW, LW)], r.o_out)],
    ]

    def flush_copies(i):
        return [
            pltpu.make_async_copy(src, dst, r.lsem.at[len(loads) + i + n]) for n, (src, dst) in enumerate(flush[i])
        ]

    by_row = [True, False, True]

    def part(ref, i, q):
        if by_row[i]:
            size = ref.shape[0] // NX
            return ref.at[pl.ds(pl.multiple_of(q * size, size), size)]
        size = ref.shape[1] // NX
        return ref.at[:, pl.ds(pl.multiple_of(q * size, size), size)]

    def w1(l):
        for n0, n in tiles(D):
            cols = slice(n0, n0 + n)
            for g in range(2):
                r.Xgu[l, g * HW : (g + 1) * HW, cols] = sum(
                    dot_tn(r.gub[l, k, :, g * HP : (g + 1) * HP], flat(r.norm.at[l, k], cols))
                    for k in range(CHUNKS)
                )[:HW].astype(BF)
        for n0, n in tiles(D):
            r.Xdn[l, :, n0 : n0 + n] = sum(
                dot_tn(
                    r.hid[l, k],
                    outbf(l, k)[:, n0 : n0 + n] if l == 1 else flat(outbf(l, k), slice(n0, n0 + n)),
                )
                for k in range(CHUNKS)
            )[:HW].astype(BF)

    def w2_0():
        for n0, n in tiles(D):
            cols = slice(n0, n0 + n)
            r.Xcv[0, : 3 * LW, cols] = sum(
                dot_tn(r.pbf[k], r.tok[k, :, cols]) for k in range(CHUNKS)
            ).astype(BF)
            r.Xcv[0, 3 * LW :, cols] = sum(
                dot_tn(r.mixed[k], flat(r.rb.at[0, k], cols)) for k in range(CHUNKS)
            ).astype(BF)

    def w2_1():
        await_bytes(r.pm.at[pl.ds(0, NW - 1)], r.pmsem.at[1])
        for k in range(CHUNKS):
            ag_wait(ag_id["u", k], r.u1.at[k])
            ag_wait(ag_id["r", 1, k], r.rb.at[1, k])
        pm = [r.pm[:, k * ROWS : (k + 1) * ROWS].reshape(T, 4 * LW) for k in range(CHUNKS)]
        for n0, n in tiles(D):
            cols = slice(n0, n0 + n)
            r.Xcv[1, : 3 * LW, cols] = sum(
                dot_tn(pm[k][:, : 3 * LW], flat(r.u1.at[k], cols)) for k in range(CHUNKS)
            ).astype(BF)
            r.Xcv[1, 3 * LW :, cols] = sum(
                dot_tn(pm[k][:, 3 * LW :], flat(r.rb.at[1, k], cols)) for k in range(CHUNKS)
            ).astype(BF)

    def core_send(l, i):
        @pl.when(c != l)
        def _():
            remote(X[i].at[l], Y[i], r.csend.at[i], r.crecv.at[i], core_peer).start()

    def x_reduce(l, i):
        @pl.when(c == l)
        def _():
            await_bytes(Y[i], r.crecv.at[i])
            rows_total = Y[i].shape[0]

            def add(rows):
                X[i][l, rows] = (X[i][l, rows].astype(F32) + Y[i][rows].astype(F32)).astype(BF)

            row_loop(rows_total, 32, add)
            mine = R[i].at[x]
            for j in range(1, NX):
                dev = x_peer(j)
                remote(
                    part(X[i].at[l], i, dev[1]), mine, r.xsend.at[i], r.xrecv.at[i], dev
                ).start()

    def x_gather(l, i):
        @pl.when(c == l)
        def _():
            await_bytes(R[i].at[pl.ds(0, NX - 1)], r.xrecv.at[i])
            src = part(X[i].at[l], i, x)
            R[i][x] = src[...]
            dst = part(Y[i], i, x)
            rows_total = dst.shape[0]

            def add(rows):
                total = R[i][0, rows].astype(F32)
                for j in range(1, NX):
                    total = total + R[i][j, rows].astype(F32)
                dst[rows] = total.astype(BF)

            row_loop(rows_total, 16, add)
            for j in range(1, NX):
                remote(dst, dst, r.vsend.at[i], r.vrecv.at[i], x_peer(j)).start()

    def x_finish(l, i):
        @pl.when(c == l)
        def _():
            await_bytes(R[i].at[pl.ds(0, NX - 1)], r.vrecv.at[i])
            await_bytes(R[i].at[pl.ds(0, NX - 1)], r.xsend.at[i])
            await_bytes(R[i].at[pl.ds(0, NX - 1)], r.vsend.at[i])
            for cp in flush_copies(i):
                cp.start()

        @pl.when(c != l)
        def _():
            await_bytes(Y[i], r.csend.at[i])

    GR = D // 128

    def gain_send(l):
        st = r.gst.at[l]
        for i in range(GR):
            st[0, i : i + 1] = r.gacc[l, :, i * 128 : (i + 1) * 128]
        gain = st[0, 0:GR]
        for i in range(NW):
            st[i, 0:GR] = gain
            st[i, GR:] = jnp.zeros((8, 128), F32)
            if l == 1:
                st[i, GR : GR + 3, :LW] = r.tap1g[:, i * LW : (i + 1) * LW]
        mine = r.gex.at[l, w]
        mine[...] = st[w]

        def it(i, carry):
            dev = wa_peer(i)
            remote(st.at[dev[2]], mine, r.gsend.at[l], r.grecv.at[l], dev).start()
            return carry

        lax.fori_loop(1, NW, it, 0)

    def gain_recv(l):
        await_bytes(r.gex.at[l, pl.ds(0, NW - 1)], r.grecv.at[l])
        total = r.gex[l, 0]
        for i in range(1, NW):
            total = total + r.gex[l, i]
        r.sm[l] = total

    def small_send(l):
        if l == 0:
            r.sm[0, GR:] = r.sm[0, GR:] + r.tacc[...]

        @pl.when(c != l)
        def _():
            remote(r.sm.at[l], r.smY, r.csend.at[3], r.crecv.at[3], core_peer).start()

    def small_x(l):
        @pl.when(c == l)
        def _():
            await_bytes(r.smY, r.crecv.at[3])
            mine = r.smR.at[x]
            mine[...] = r.sm[l] + r.smY[...]
            for j in range(1, NX):
                remote(mine, mine, r.xsend.at[3], r.xrecv.at[3], x_peer(j)).start()

    def small_finish(l):
        @pl.when(c == l)
        def _():
            await_bytes(r.smR.at[pl.ds(0, NX - 1)], r.xrecv.at[3])
            total = r.smR[0]
            for j in range(1, NX):
                total = total + r.smR[j]
            for i in range(GR):
                r.o_gain[:, i * 128 : (i + 1) * 128] = total[i : i + 1]
            r.o_tap[...] = total[GR : GR + 3, :LW]
            await_bytes(r.smR.at[pl.ds(0, NX - 1)], r.xsend.at[3])

        @pl.when(c != l)
        def _():
            await_bytes(r.smY, r.csend.at[3])

    A, B = 0, 1
    AB, BA = (0, 1), (1, 0)
    s1(0, A)
    s1(0, B)
    gather_wa()
    s2(0, A)
    s2(0, B)
    gather_mid()
    mids("rs", 0, "a", AB)
    gather_x(0)
    s3(0, A)
    s3(0, B)
    gather_x(1)
    mids("ag", 0, "n", AB)
    s4(0, A)
    s4(0, B)
    gather_x(2)
    prep_cot(A)
    mids("rs", 0, "b", AB)
    gather_core(0)
    gather_x(3)
    prep_cot(B)
    s5(0, A)
    s5(0, B)
    gather_core(1)
    f1a()
    gather_core(3)
    f1b()
    mids("ag", 1, "n", AB)
    u_start()
    s4(1, A)
    s4(1, B)
    t1(1, B)
    mids("rs", 1, "b", AB)
    t1(1, A)
    mids("ag", 1, "u", AB)
    mids("rs", 1, "c", BA)
    w1(1)
    t2(1, B)
    t2(1, A)
    b1a()
    core_send(1, 0)
    core_send(1, 1)
    b1b()
    s5(1, A)
    s5(1, B)
    mids("ag", 0, "g", BA)
    gain_send(1)
    b1_exchange()
    x_reduce(1, 0)
    x_reduce(1, 1)
    t1(0, B)
    t1(0, A)
    w1(0)
    core_send(0, 0)
    core_send(0, 1)
    mids("rs", 0, "c", BA)
    mids("ag", 1, "r", BA)
    gain_recv(1)
    small_send(1)
    x_gather(1, 0)
    x_gather(1, 1)
    x_reduce(0, 0)
    x_reduce(0, 1)
    t2(0, B)
    t2(0, A)
    mids("ag", 0, "r", BA)
    gain_send(0)
    w2_1()
    core_send(1, 2)
    t3(0, B)
    t3(0, A)
    x_reduce(1, 2)
    small_x(1)
    x_gather(0, 0)
    x_gather(0, 1)
    t4(0, B)
    t4(0, A)
    w2_0()
    core_send(0, 2)
    mids("rs", 0, "d", BA)
    x_reduce(0, 2)
    gain_recv(0)
    small_send(0)
    small_x(0)
    x_gather(1, 2)
    t5(0, B)
    t5(0, A)
    for i in range(3):
        x_finish(1, i)
    x_gather(0, 2)
    small_finish(1)
    for i in range(3):
        x_finish(0, i)
    small_finish(0)
    gather_close()
    await_bytes(r.pm.at[pl.ds(0, NW - 1)], r.pmsem.at[0])

    for sems, staging, target, out in ((0, r.lost, r.lo, r.o_layer), (1, r.ligst, r.ig, r.o_grad)):
        for k in range(CHUNKS):
            await_bytes(staging.at[0, k], r.orecv.at[sems, k])
            await_bytes(staging.at[0, k], r.osend.at[sems, k])
        out[...] = target[...]
    for n, buf in ag_sent:
        for i in range(2):
            await_bytes(ag_first(buf), r.ags.at[n, i])
            await_bytes(ag_second(buf), r.ags.at[n, 2 + i])
    for uses in stage_use:
        for n, buf in uses[-2:]:
            stage_sent(n, buf)
        for n, buf in uses:
            await_bytes(r.rwa.at[n, pl.ds(0, NZ - 1)], r.rss.at[n, 2])
            await_bytes(r.rwb.at[n, pl.ds(0, NY - 1)], r.rss.at[n, 3])
    for l in range(2):
        await_bytes(r.gex.at[l, pl.ds(0, NW - 1)], r.gsend.at[l])
    for fsem, fbuf, bsem, bbuf, no_next, no_prev in (
        (r.hsend, r.hs, r.hgsend, r.hgs, last * c, first * (1 - c)),
        (r.h1send, r.h1s, r.hg1send, r.hg1b, end * c, begin * (1 - c)),
    ):
        for k in range(CHUNKS):

            def fwd(k=k, fsem=fsem, fbuf=fbuf):
                await_bytes(fbuf.at[k], fsem.at[k])

            def bwd(k=k, bsem=bsem, bbuf=bbuf):
                await_bytes(bbuf.at[k], bsem.at[k])

            if k == CHUNKS - 1:
                pl.when(no_next == 0)(fwd)
            else:
                fwd()
            if k == 0:
                pl.when(no_prev == 0)(bwd)
            else:
                bwd()
    for cp in wcopies:
        cp.wait_send()
    for i in range(3):
        for cp in flush_copies(i):
            cp.wait()


def body(NX, NW, tokens, cotangent, in_weight, conv_weight, out_weight, norm_gain, gate_up_weight, down_weight):
    micro, T, D = tokens.shape
    LW = conv_weight.shape[2]
    HW = gate_up_weight.shape[3]
    HP = -(-HW // 128) * 128
    w_small = jnp.concatenate(
        [norm_gain, jnp.pad(conv_weight[0], ((0, 4), (0, D - LW)))], 0
    )
    GR = D // 128
    L, K = 2, CHUNKS
    vmem = pltpu.VMEM
    dma = pltpu.SemaphoreType.DMA
    n_ag, n_rs = 6 * K, 6 * K
    NY = NZ = next(i for i in range(1, NW + 1) if i * i >= NW)
    plane = (NZ, NY, ROWS, D)
    ins = dict(
        tokens=tokens, cotangent=cotangent, w_in=in_weight[0].transpose(1, 2, 0), w_out=out_weight[0],
        w_gu=gate_up_weight[0].transpose(1, 2, 0), w_dn=down_weight[0], w_small=w_small
    )
    anyspec = pl.BlockSpec(memory_space=pl.ANY)
    vspec = pl.BlockSpec(memory_space=pltpu.VMEM)
    shape = jax.ShapeDtypeStruct
    outs = dict(
        o_layer=(shape((micro, ROWS, D), BF), vspec),
        o_grad=(shape((micro, ROWS, D), F32), vspec),
        o_in=(shape((3 * LW, D), BF), anyspec),
        o_out=(shape((LW, D), BF), anyspec),
        o_gu=(shape((2 * HW, D), BF), anyspec),
        o_dn=(shape((HW, D), BF), anyspec),
        o_gain=(shape((1, D), F32), vspec),
        o_tap=(shape((3, LW), F32), vspec),
    )
    scratch = dict(
        Cown=vmem((L, 4, LW, D), BF), Cfull=vmem((4, NZ, NY, LW, D), BF),
        Wgu=vmem((L, 2, HP, D), BF), Wdn=vmem((L, HP, D), BF), Wsm=vmem((L, 8, D), F32),
        tok=vmem((K, T, D), BF), cot=vmem((K, T, D), F32), cotb=vmem((K, T, D), BF),
        projB=vmem((K, T, LW), F32), projC=vmem((K, T, LW), F32), projX=vmem((K, T, LW), F32),
        gp=vmem((K, T + 8, LW), F32), conv=vmem((K, T, LW), F32), mixed=vmem((K, T, LW), BF),
        gu=vmem((L, K, T, 2 * HP), F32), hg=vmem((K, T, HP), F32), hid=vmem((L, K, T, HP), BF),
        gub=vmem((L, K, T, 2 * HP), BF), pbf=vmem((K, T, 3 * LW), BF),
        res=vmem((L, K, ROWS, D), F32), rg=vmem((L, K, ROWS, D), F32), g0own=vmem((K, ROWS, D), F32),
        cvg=vmem((K, T + 8, LW), F32),
        norm=vmem((L, K) + plane, BF), u1=vmem((K,) + plane, BF), rb=vmem((L, K) + plane, BF), gbf=vmem((K,) + plane, BF),
        stage=vmem((K, 2) + plane, BF), rva=vmem((n_rs, NY, NZ, ROWS, D // 2), BF), rvb=vmem((n_rs, NZ, NY, ROWS, D // 2), BF),
        rsa=vmem((n_rs, NZ, ROWS, D // 2), BF), rsb=vmem((n_rs, NY, ROWS, D // 2), BF),
        rwa=vmem((n_rs, NZ, ROWS, D // 2), BF), rwb=vmem((n_rs, NY, ROWS, D // 2), BF),
        hs=vmem((K, 16, LW), BF), hb=vmem((K, 16, LW), BF), hgs=vmem((K, 8, LW), F32), hgb=vmem((K, 8, LW), F32),
        proj1=vmem((3, K * ROWS, D), F32), gp1=vmem((K, ROWS + 8, D), F32), conv1=vmem((K, ROWS, D), F32),
        mixed1=vmem((K * ROWS, D), BF), cv1=vmem((K, ROWS + 8, D), F32), pbf1=vmem((K * ROWS, 3 * D), BF),
        h1s=vmem((K, ROWS, D), BF), h1b=vmem((K, ROWS, D), BF), hg1b=vmem((K, 8, D), F32),
        trow=vmem((3, D), F32), tap1g=vmem((3, D), F32), taps1=vmem((NW, 8, 128), F32),
        pms=vmem((NW, K * ROWS, 4 * LW), BF), pm=vmem((NW, K * ROWS, 4 * LW), BF),
        lost=vmem((L, K, ROWS, D), BF), ligst=vmem((L, K, ROWS, D), F32),
        lo=vmem((micro, ROWS, D), BF), ig=vmem((micro, ROWS, D), F32),
        Xgu=vmem((L, 2 * HW, D), BF), Xdn=vmem((L, HW, D), BF), Xcv=vmem((L, 4 * LW, D), BF),
        Ygu=vmem((2 * HW, D), BF), Ydn=vmem((HW, D), BF), Ycv=vmem((4 * LW, D), BF),
        Rgu=vmem((NX, 2 * HW // NX, D), BF), Rdn=vmem((NX, HW, D // NX), BF), Rcv=vmem((NX, 4 * LW // NX, D), BF),
        gacc=vmem((L, 1, D), F32), tacc=vmem((8, 128), F32), gst=vmem((L, NW, GR + 8, 128), F32),
        gex=vmem((L, NW, GR + 8, 128), F32), sm=vmem((L, GR + 8, 128), F32),
        smY=vmem((GR + 8, 128), F32), smR=vmem((NX, GR + 8, 128), F32),
        lsem=dma((16,)), wsend=dma((5,)), wrecv=dma((5,)), ags=dma((n_ag, 4)), agr=dma((n_ag, 4)),
        rss=dma((n_rs, 4)), rsr=dma((n_rs, 4)), hsend=dma((K,)), hrecv=dma((K,)), hgsend=dma((K,)), hgrecv=dma((K,)),
        h1send=dma((K,)), h1recv=dma((K,)), hg1send=dma((K,)), hg1recv=dma((K,)), pmsem=dma((2,)),
        gwsem=dma((11,)), gxs=dma((4,)), gxr=dma((4,)), gcs=dma((4,)), gcr=dma((4,)),
        osend=dma((2, K)), orecv=dma((2, K)), csend=dma((4,)), crecv=dma((4,)), xsend=dma((4,)), xrecv=dma((4,)),
        vsend=dma((3,)), vrecv=dma((3,)), gsend=dma((L,)), grecv=dma((L,)),
    )
    names = tuple(ins) + tuple(outs) + tuple(scratch)
    layer, grad, g_in, g_out, g_gu, g_dn, g_gain, g_tap = pl.pallas_call(
        functools.partial(kernel, (NX, NW, T, D, LW, HW, HP), names),
        out_shape=tuple(o[0] for o in outs.values()),
        in_specs=[anyspec] * len(ins),
        out_specs=tuple(o[1] for o in outs.values()),
        scratch_shapes=list(scratch.values()),
        compiler_params=pltpu.CompilerParams(
            collective_id=0, has_side_effects=True, vmem_limit_bytes=63 << 20
        ),
    )(*ins.values())
    return (
        layer[None],
        grad[None],
        g_in.reshape(3, LW, D).transpose(2, 0, 1).astype(F32)[None],
        g_tap[None],
        g_out.astype(F32)[None],
        g_gain,
        g_gu.reshape(2, HW, D).transpose(2, 0, 1).astype(F32)[None],
        g_dn.astype(F32)[None],
    )


def solution(mesh):
    in_specs = (
        P(None, "seq", None),
        P(None, "seq", None),
        P("section", None, None, "wa"),
        P("section", None, "wa"),
        P("section", "wa", None),
        P("section", None),
        P("section", None, None, "wa"),
        P("section", "wa", None),
    )
    out_specs = (
        P("section", None, ("seq", "wa"), None),
        P("section", None, ("seq", "wa"), None),
        P("section", None, None, "wa"),
        P("section", None, "wa"),
        P("section", "wa", None),
        P("section", None),
        P("section", None, None, "wa"),
        P("section", "wa", None),
    )
    fn = functools.partial(body, mesh.shape["seq"], mesh.shape["wa"])
    return jax.shard_map(fn, mesh=mesh, in_specs=in_specs, out_specs=out_specs, check_vma=False)
```

```python
import functools
import types

import jax
import jax.numpy as jnp
from jax import lax
from jax.experimental import pallas as pl
from jax.experimental.pallas import tpu as pltpu
from jax.sharding import PartitionSpec as P

EPSILON = 1e-05
MESH = pl.DeviceIdType.MESH
BF = jnp.bfloat16
F32 = jnp.float32
ROWS = 16
CHUNKS = 2


def dot_nn(a, b):
    return jnp.dot(a, b, preferred_element_type=F32)


def dot_nt(a, b):
    return lax.dot_general(a, b, (((1,), (1,)), ((), ())), preferred_element_type=F32)


def dot_tn(a, b):
    return lax.dot_general(a, b, (((0,), (0,)), ((), ())), preferred_element_type=F32)


def tiles(total, size=256):
    return [(start, min(size, total - start)) for start in range(0, total, size)]


def row_loop(total, step, fn):
    def it(i, carry):
        fn(pl.ds(pl.multiple_of(i * step, step), step))
        return carry

    lax.fori_loop(0, total // step, it, 0)


def kernel(cfg, names, *refs):
    NX, NW, T, D, LW, HW, HP = cfg
    r = types.SimpleNamespace(**dict(zip(names, refs, strict=True)))
    c = lax.axis_index("section")
    x = lax.axis_index("seq")
    w = lax.axis_index("wa")
    last = (x + 1) // NX
    first = (NX - x) // NX
    own = pl.ds(pl.multiple_of(w * ROWS, ROWS), ROWS)
    core_peer = (1 - c, x, w)
    NY = NZ = next(i for i in range(1, NW + 1) if i * i >= NW)
    z = w // NY
    y = w - z * NY
    LO, HI = pl.ds(0, D // 2), pl.ds(D // 2, D // 2)
    w_last = (w + 1) // NW
    w_first = (NW - w) // NW
    end = last * w_last
    begin = first * w_first
    next_dev = (c + end * (1 - 2 * c), lax.rem(x + w_last, NX), lax.rem(w + 1, NW))
    prev_dev = (c + begin * (1 - 2 * c), lax.rem(x + NX - w_first, NX), lax.rem(w + NW - 1, NW))

    def y_at(i):
        return lax.rem(y + i, NY)

    def z_at(i):
        return lax.rem(z + i, NZ)

    def y_peer(i):
        return (c, x, z * NY + y_at(i))

    def z_peer(i):
        return (c, x, z_at(i) * NY + y)

    def flat(ref, *cols):
        value = ref[(slice(None),) * 3 + cols] if cols else ref[...]
        return value.reshape(T, value.shape[-1])

    def wa_peer(i):
        return (c, x, lax.rem(w + i, NW))

    def x_peer(i):
        return (c, lax.rem(x + i, NX), w)

    def remote(src, dst, send, recv, dev):
        return pltpu.make_async_remote_copy(
            src_ref=src, dst_ref=dst, send_sem=send, recv_sem=recv, device_id=dev, device_id_type=MESH
        )

    def await_bytes(ref, sem):
        pltpu.make_async_copy(ref, ref, sem).wait()

    loads = []

    def load(src, dst):
        cp = pltpu.make_async_copy(src, dst, r.lsem.at[len(loads)])
        cp.start()
        loads.append(cp)
        return len(loads) - 1

    wpairs = [
        (r.w_in, r.Cown.at[c, pl.ds(0, 3)]),
        (r.Wsm.at[c], r.Wsm.at[c]),
        (r.w_gu, r.Wgu.at[c, :, pl.ds(0, HW)]),
        (r.w_dn, r.Wdn.at[c, pl.ds(0, HW)]),
        (r.w_out, r.Cown.at[c, 3]),
    ]
    l_tok = [load(r.tokens.at[c], r.tok.at[0]), None]
    l_w = [load(*wpairs[0]), None]
    l_tok[1] = load(r.tokens.at[2 + c], r.tok.at[1])
    l_w += [load(*p) for p in wpairs[2:]]
    l_cot = [load(r.cotangent.at[2 * k + c], r.cot.at[k]) for k in range(CHUNKS)]

    r.Wsm[c] = jnp.zeros((8, D), F32)
    r.Wsm[c, 0:1] = r.w_gain[...]
    for j in range(3):
        r.Wsm[c, j + 1 : j + 2, :LW] = r.w_conv[j]

    bar = pltpu.get_barrier_semaphore()

    def sig(dev):
        pl.semaphore_signal(bar, inc=1, device_id=dev, device_id_type=MESH)

    sig(core_peer)

    def sig_wa(i, carry):
        sig(wa_peer(i))
        return carry

    lax.fori_loop(1, NW, sig_wa, 0)
    for i in range(1, NX):
        sig(x_peer(i))
    sig((1 - c, lax.rem(x + 1, NX), w))
    sig((1 - c, lax.rem(x + NX - 1, NX), w))
    sig(next_dev)
    sig(prev_dev)
    if HP > HW:
        for l in range(2):
            r.Wdn[l, HW:] = jnp.zeros((HP - HW, D), BF)
            r.Wgu[l, :, HW:] = jnp.zeros((2, HP - HW, D), BF)
    r.gacc[...] = jnp.zeros(r.gacc.shape, F32)
    r.tacc[...] = jnp.zeros(r.tacc.shape, F32)
    pl.semaphore_wait(bar, (NW - 1) + (NX - 1) + 5)

    wcopies = []
    for i, (src, dst) in enumerate(wpairs):
        cp = remote(src, dst, r.wsend.at[i], r.wrecv.at[i], core_peer)
        cp.start()
        wcopies.append(cp)
    wready = set()

    def need_w(i):
        if i not in wready:
            wready.add(i)
            if l_w[i] is not None:
                loads[l_w[i]].wait()
            wcopies[i].wait_recv()

    full = r.Cfull
    HALF = D // 2
    LQ = LW // NX
    xrows = pl.ds(pl.multiple_of(x * LQ, LQ), LQ)
    clanes = pl.ds(pl.multiple_of(c * HALF, HALF), HALF)
    la, lb = (pl.ds(pl.multiple_of(c * HALF + h, HALF // 2), HALF // 2) for h in (0, HALF // 2))
    first_a, first_b = full.at[:, 0, 0 : NY - 1, xrows, la], full.at[:, 0 : NZ - 1, 0, xrows, lb]
    second_a, second_b = full.at[:, 0 : NZ - 1, :, xrows, la], full.at[:, :, 0 : NY - 1, xrows, lb]

    def gather_wa():
        need_w(0)
        need_w(1)
        need_w(4)
        local = pltpu.make_async_copy(
            r.Cown.at[1, :, xrows, clanes], full.at[:, z, y, xrows, clanes], r.gwsem.at[0]
        )
        local.start()
        for lanes, peer, count, sem in ((la, y_peer, NY, 1), (lb, z_peer, NZ, 5)):
            for i in range(1, count):
                remote(
                    r.Cown.at[1, :, xrows, lanes], full.at[:, z, y, xrows, lanes],
                    r.gwsem.at[sem], r.gwsem.at[sem + 1], peer(i),
                ).start()
        tap = r.Wsm.at[1, :, pl.ds(0, 128)]
        tap_dst = r.taps1.at[w]
        tap_dst[...] = tap[...]

        def it(i, carry):
            remote(tap, tap_dst, r.gwsem.at[3], r.gwsem.at[4], wa_peer(i)).start()
            return carry

        lax.fori_loop(1, NW, it, 0)
        local.wait()

    def gather_mid():
        await_bytes(first_a, r.gwsem.at[2])
        piece = full.at[:, z, :, xrows, la]
        for i in range(1, NZ):
            remote(piece, piece, r.gwsem.at[7], r.gwsem.at[8], z_peer(i)).start()
        await_bytes(first_b, r.gwsem.at[6])
        piece = full.at[:, :, y, xrows, lb]
        for i in range(1, NY):
            remote(piece, piece, r.gwsem.at[9], r.gwsem.at[10], y_peer(i)).start()

    def gather_x(p):
        if p == 0:
            await_bytes(second_a, r.gwsem.at[8])
            await_bytes(second_b, r.gwsem.at[10])
        piece = full.at[p, :, :, xrows, clanes]
        for j in range(1, NX):
            remote(piece, piece, r.gxs.at[p], r.gxr.at[p], x_peer(j)).start()

    def gather_core(p):
        await_bytes(full.at[p, :, :, pl.ds(0, (NX - 1) * LQ), clanes], r.gxr.at[p])
        piece = full.at[p, :, :, :, clanes]
        remote(piece, piece, r.gcs.at[p], r.gcr.at[p], core_peer).start()

    def gather_done(p):
        await_bytes(full.at[p, :, :, :, clanes], r.gcr.at[p])

    def gather_close():
        for ref, sem in ((first_a, 1), (first_b, 5), (second_a, 7), (second_b, 9)):
            await_bytes(ref, r.gwsem.at[sem])
        await_bytes(r.taps1.at[pl.ds(0, NW - 1)], r.gwsem.at[3])
        for p in range(4):
            await_bytes(full.at[p, :, :, pl.ds(0, (NX - 1) * LQ), clanes], r.gxs.at[p])
            await_bytes(full.at[p, :, :, :, clanes], r.gcs.at[p])

    counts = {"ag": 0, "rs": 0}
    ag_sent, rs_sent = [], []

    def ag_start(buf):
        n = counts["ag"]
        counts["ag"] += 1
        lo, hi = buf.at[z, y, :, LO], buf.at[z, y, :, HI]
        for i in range(1, NY):
            remote(lo, lo, r.ags.at[n, 0], r.agr.at[n, 0], y_peer(i)).start()
            remote(hi, hi, r.ags.at[n, 1], r.agr.at[n, 1], z_peer(i)).start()
        ag_sent.append((n, buf))
        return n

    def ag_first(buf):
        return buf.at[0, pl.ds(0, NY - 1), :, LO]

    def ag_second(buf):
        return buf.at[pl.ds(0, NZ - 1), :, :, LO]

    def ag_mid(n, buf):
        lo, hi = buf.at[z, :, :, LO], buf.at[:, y, :, HI]
        await_bytes(ag_first(buf), r.agr.at[n, 0])
        for i in range(1, NZ):
            remote(lo, lo, r.ags.at[n, 2], r.agr.at[n, 2], z_peer(i)).start()
        await_bytes(ag_first(buf), r.agr.at[n, 1])
        for i in range(1, NY):
            remote(hi, hi, r.ags.at[n, 3], r.agr.at[n, 3], y_peer(i)).start()

    def ag_wait(n, buf):
        for i in (2, 3):
            await_bytes(ag_second(buf), r.agr.at[n, i])

    stage_use = [[], []]

    def stage_get(k):
        uses = stage_use[k]
        slot = len(uses) % 2
        if len(uses) >= 2:
            stage_sent(*uses[-2])
        return r.stage.at[k, slot]

    def stage_sent(n, buf):
        for i in (0, 1):
            await_bytes(ag_second(buf), r.rss.at[n, i])

    def rs_start(k, buf):
        n = counts["rs"]
        counts["rs"] += 1
        for i in range(1, NY):
            remote(
                buf.at[:, y_at(i), :, LO], r.rva.at[n, y], r.rss.at[n, 0], r.rsr.at[n, 0], y_peer(i)
            ).start()
            remote(
                buf.at[z_at(i), :, :, HI], r.rvb.at[n, z], r.rss.at[n, 1], r.rsr.at[n, 1], z_peer(i)
            ).start()
        stage_use[k].append((n, buf))
        return n

    def rs_mid(n, k):
        buf = dict(stage_use[k])[n]
        sa, sb = r.rsa.at[n], r.rsb.at[n]
        await_bytes(r.rva.at[n, pl.ds(0, NY - 1)], r.rsr.at[n, 0])
        total = buf[:, y, :, LO].astype(F32)
        for i in range(1, NY):
            total = total + r.rva[n, y_at(i)].astype(F32)
        sa[...] = total.astype(BF)
        for i in range(1, NZ):
            remote(sa.at[z_at(i)], r.rwa.at[n, z], r.rss.at[n, 2], r.rsr.at[n, 2], z_peer(i)).start()
        await_bytes(r.rvb.at[n, pl.ds(0, NZ - 1)], r.rsr.at[n, 1])
        total = buf[z, :, :, HI].astype(F32)
        for i in range(1, NZ):
            total = total + r.rvb[n, z_at(i)].astype(F32)
        sb[...] = total.astype(BF)
        for i in range(1, NY):
            remote(sb.at[y_at(i)], r.rwb.at[n, y], r.rss.at[n, 3], r.rsr.at[n, 3], y_peer(i)).start()

    def rs_sum(n):
        await_bytes(r.rwa.at[n, pl.ds(0, NZ - 1)], r.rsr.at[n, 2])
        lo = r.rsa[n, z].astype(F32)
        for i in range(1, NZ):
            lo = lo + r.rwa[n, z_at(i)].astype(F32)
        await_bytes(r.rwb.at[n, pl.ds(0, NY - 1)], r.rsr.at[n, 3])
        hi = r.rsb[n, y].astype(F32)
        for i in range(1, NY):
            hi = hi + r.rwb[n, y_at(i)].astype(F32)
        return jnp.concatenate([lo, hi], 1)

    def mids(kind, l, name, ks):
        for k in ks:
            if kind == "rs":
                rs_mid(rs_id[name, l, k], k)
            else:
                key, buf = {
                    "n": (("n", l, k), r.norm.at[l, k]),
                    "u": (("u", k), r.u1.at[k]),
                    "r": (("r", l, k), r.rb.at[l, k]),
                    "g": (("g", k), r.gbf.at[k]),
                }[name]
                ag_mid(ag_id[key], buf)

    rs_id, ag_id = {}, {}

    def u_of(l, k):
        return r.tok.at[k] if l == 0 else r.u1.at[k]

    hcopy = {}

    w0 = r.Cown.at[0]

    def put(ref, n0, n, value):
        ref[:, :, :, n0 : n0 + n] = value.astype(BF).reshape(NZ, NY, ROWS, n)

    def s1(l, k):
        u = u_of(l, k)
        loads[l_tok[k]].wait()
        need_w(0)
        projected = dot_nt(u[...], w0[0:3].reshape(3 * LW, D))
        b_part = projected[:, :LW]
        x_part = projected[:, 2 * LW :]
        r.projB[k] = b_part
        r.projC[k] = projected[:, LW : 2 * LW]
        r.projX[k] = x_part
        gated = (b_part * x_part).astype(BF)
        r.gp[k, pl.ds(8, T)] = gated.astype(F32)
        r.hs[k] = gated[T - 16 :]

        slot = k + last * c

        def send():
            remote(
                r.hs.at[k],
                r.hb.at[slot],
                r.hsend.at[k],
                r.hrecv.at[slot],
                (c + last * (1 - 2 * c), lax.rem(x + 1, NX), w),
            ).start()

        if k == CHUNKS - 1:
            pl.when(last * c == 0)(send)
        else:
            send()

    def s2(l, k):
        def get():
            await_bytes(r.hb.at[k], r.hrecv.at[k])

        def zero():
            r.hb[k] = jnp.zeros((16, LW), BF)

        if k == 0:
            none = first * (1 - c)
            pl.when(none == 0)(get)
            pl.when(none == 1)(zero)
        else:
            get()
        need_w(1)
        need_w(4)
        r.gp[k, pl.ds(0, 8)] = r.hb[k].astype(F32)[8:]
        taps = r.Wsm[l]
        conv = (
            taps[1:2, :LW] * r.gp[k, pl.ds(6, T)]
            + taps[2:3, :LW] * r.gp[k, pl.ds(7, T)]
            + taps[3:4, :LW] * r.gp[k, pl.ds(8, T)]
        )
        r.conv[k] = conv
        r.mixed[k] = (r.projC[k] * conv).astype(BF)
        buf = stage_get(k)
        for n0, n in tiles(D):
            put(buf, n0, n, dot_nn(r.mixed[k], w0[3, :, n0 : n0 + n]))
        rs_id["a", l, k] = rs_start(k, buf)

    def inv_rms(res):
        return lax.rsqrt(jnp.mean(res * res, -1, keepdims=True) + EPSILON)

    def s3(l, k):
        res = r.tok[k, own].astype(F32) + rs_sum(rs_id["a", l, k])
        r.res[l, k] = res
        buf = r.norm.at[l, k]
        buf[z, y] = (res * inv_rms(res) * r.Wsm[l, 0:1]).astype(BF)
        ag_id["n", l, k] = ag_start(buf)

    def s4(l, k):
        buf = r.norm.at[l, k]
        ag_wait(ag_id["n", l, k], buf)
        need_w(2)
        need_w(3)
        gu = r.gu.at[l, k]
        for g in range(2):
            gu[:, g * HP : (g + 1) * HP] = dot_nt(flat(buf), r.Wgu[l, g])

        def act(rows):
            gate = gu[rows, :HP]
            up = gu[rows, HP:]
            r.hid[l, k, rows] = (gate * jax.nn.sigmoid(gate) * up).astype(BF)

        row_loop(T, 32, act)

    def s4_down(l, k):
        st = stage_get(k)
        for n0, n in tiles(D):
            put(st, n0, n, dot_nn(r.hid[l, k], r.Wdn[l, :, n0 : n0 + n]))
        rs_id["b", l, k] = rs_start(k, st)

    def emit(l, k, value, staging, target, sems):
        staging[l, k] = value

        @pl.when(c == l)
        def _():
            target[2 * k + c] = value

        @pl.when(c != l)
        def _():
            remote(
                staging.at[l, k],
                target.at[2 * k + c],
                r.osend.at[sems, k],
                r.orecv.at[sems, k],
                core_peer,
            ).start()

    def s5(l, k):
        rows = (r.res[l, k] + rs_sum(rs_id["b", l, k])).astype(BF)
        if l == 0:
            r.u1[k, z, y] = rows
        emit(l, k, rows, r.lost, r.lo, 0)

    def outbf(l, k):
        return r.cotb.at[k] if l == 1 else r.gbf.at[k]

    def prep_cot(k):
        loads[l_cot[k]].wait()

        def cast(rows):
            r.cotb[k, rows] = r.cot[k, rows].astype(BF)

        row_loop(T, 32, cast)

    def t1(l, k):
        ob = outbf(l, k)
        if l == 0:
            ag_wait(ag_id["g", k], ob)
        hg = r.hg.at[k]
        for n0, n in tiles(HP):
            hg[:, n0 : n0 + n] = dot_nt(ob[...] if l == 1 else flat(ob), r.Wdn[l, n0 : n0 + n])
        gu = r.gu.at[l, k]
        gub = r.gub.at[l, k]

        def act(rows):
            gate = gu[rows, :HP]
            up = gu[rows, HP:]
            h = hg[rows]
            s = jax.nn.sigmoid(gate)
            gub[rows, :HP] = (h * up * (s * (1.0 + gate * (1.0 - s)))).astype(BF)
            gub[rows, HP:] = (h * (gate * s)).astype(BF)

        row_loop(T, 32, act)
        st = stage_get(k)
        for n0, n in tiles(D):
            put(st, n0, n, dot_nn(gub[...], r.Wgu[l, :, :, n0 : n0 + n].reshape(2 * HP, n)))
        rs_id["c", l, k] = rs_start(k, st)

    def t2(l, k):
        ng = rs_sum(rs_id["c", l, k])
        res = r.res[l, k]
        inv = inv_rms(res)
        g = r.cot[k, own] if l == 1 else r.g0own[k]
        r.gacc[l] = r.gacc[l] + jnp.sum(ng * res * inv, 0, keepdims=True)
        scaled = ng * r.Wsm[l, 0:1]
        rg = g + inv * scaled - res * (inv * inv * inv) * jnp.mean(scaled * res, -1, keepdims=True)
        r.rg[l, k] = rg
        buf = r.rb.at[l, k]
        buf[z, y] = rg.astype(BF)
        if l == 0:
            ag_id["r", l, k] = ag_start(buf)

    def t3(l, k):
        buf = r.rb.at[l, k]
        ag_wait(ag_id["r", l, k], buf)
        mg = dot_nt(flat(buf), w0[3])
        r.pbf[k, :, LW : 2 * LW] = (mg * r.conv[k]).astype(BF)
        cvg = mg * r.projC[k]
        r.cvg[k, pl.ds(0, T)] = cvg
        r.hgs[k] = cvg[:8]
        slot = k - first * (1 - c)

        def send():
            remote(
                r.hgs.at[k],
                r.hgb.at[slot],
                r.hgsend.at[k],
                r.hgrecv.at[slot],
                (c + first * (1 - 2 * c), lax.rem(x + NX - 1, NX), w),
            ).start()

        if k == 0:
            pl.when(first * (1 - c) == 0)(send)
        else:
            send()

    def t4(l, k):
        def get():
            await_bytes(r.hgb.at[k], r.hgrecv.at[k])

        def zero():
            r.hgb[k] = jnp.zeros((8, LW), F32)

        if k == CHUNKS - 1:
            none = last * c
            pl.when(none == 0)(get)
            pl.when(none == 1)(zero)
        else:
            get()
        e = r.cvg.at[k]
        e[pl.ds(T, 8)] = r.hgb[k]
        taps = r.Wsm[l]
        gg = (
            taps[3:4, :LW] * e[pl.ds(0, T)]
            + taps[2:3, :LW] * e[pl.ds(1, T)]
            + taps[1:2, :LW] * e[pl.ds(2, T)]
        )
        pbf = r.pbf.at[k]
        pbf[:, :LW] = (gg * r.projX[k]).astype(BF)
        pbf[:, 2 * LW :] = (gg * r.projB[k]).astype(BF)
        st = stage_get(k)
        for n0, n in tiles(D):
            put(st, n0, n, dot_nn(pbf[...], w0[0:3, :, n0 : n0 + n].reshape(3 * LW, n)))
        rs_id["d", l, k] = rs_start(k, st)
        cvg = e[pl.ds(0, T)]
        for j in range(3):
            r.tacc[j : j + 1, :LW] = r.tacc[j : j + 1, :LW] + jnp.sum(
                cvg * r.gp[k, pl.ds(6 + j, T)], 0, keepdims=True
            )

    def t5(l, k):
        rows = r.rg[l, k] + rs_sum(rs_id["d", l, k])
        emit(l, k, rows, r.ligst, r.ig, 1)

    def full_in():
        return full[0:3].reshape(3 * D, D)

    def taps_row(j):
        return jnp.concatenate([r.taps1[i, j : j + 1, :LW] for i in range(NW)], 1)

    def f1a():
        u = jnp.concatenate([r.u1[k, z, y] for k in range(CHUNKS)], 0)
        for p in range(3):
            gather_done(p)
            if p == 1:
                gather_core(2)
            r.proj1[p] = dot_nt(u, full[p].reshape(D, D))
        gated = (r.proj1[0] * r.proj1[2]).astype(BF)
        for k in range(CHUNKS):
            g = gated[k * ROWS : (k + 1) * ROWS]
            r.gp1[k, pl.ds(8, ROWS)] = g.astype(F32)
            r.h1s[k] = g
            slot = k + end * c

            def send(k=k, slot=slot):
                remote(
                    r.h1s.at[k], r.h1b.at[slot], r.h1send.at[k], r.h1recv.at[slot], next_dev
                ).start()

            if k == CHUNKS - 1:
                pl.when(end * c == 0)(send)
            else:
                send()

    def f1b():
        await_bytes(r.taps1.at[pl.ds(0, NW - 1)], r.gwsem.at[4])
        r.trow[...] = jnp.concatenate([taps_row(j + 1) for j in range(3)], 0)
        for k in range(CHUNKS):

            def get(k=k):
                await_bytes(r.h1b.at[k], r.h1recv.at[k])

            def zero(k=k):
                r.h1b[k] = jnp.zeros((ROWS, D), BF)

            if k == 0:
                none = begin * (1 - c)
                pl.when(none == 0)(get)
                pl.when(none == 1)(zero)
            else:
                get()
            r.gp1[k, pl.ds(0, 8)] = r.h1b[k].astype(F32)[8:]
            conv = sum(r.trow[j : j + 1] * r.gp1[k, pl.ds(6 + j, ROWS)] for j in range(3))
            r.conv1[k] = conv
            rows = slice(k * ROWS, (k + 1) * ROWS)
            r.mixed1[rows] = (r.proj1[1, rows] * conv).astype(BF)
        gather_done(3)
        wide = dot_nn(r.mixed1[...], full[3].reshape(D, D))
        for k in range(CHUNKS):
            res = r.u1[k, z, y].astype(F32) + wide[k * ROWS : (k + 1) * ROWS]
            r.res[1, k] = res
            buf = r.norm.at[1, k]
            buf[z, y] = (res * inv_rms(res) * r.Wsm[1, 0:1]).astype(BF)
            ag_id["n", 1, k] = ag_start(buf)

    def u_start():
        for k in range(CHUNKS):
            ag_id["u", k] = ag_start(r.u1.at[k])

    def b1a():
        rb = jnp.concatenate([r.rb[1, k, z, y] for k in range(CHUNKS)], 0)
        mg = dot_nt(rb, full[3].reshape(D, D))
        for k in range(CHUNKS):
            rows = slice(k * ROWS, (k + 1) * ROWS)
            m = mg[rows]
            cvg = m * r.proj1[1, rows]
            r.cv1[k, pl.ds(0, ROWS)] = cvg
            r.pbf1[rows, D : 2 * D] = (m * r.conv1[k]).astype(BF)
            slot = k - begin * (1 - c)

            def send(k=k, slot=slot):
                remote(
                    r.cv1.at[k, pl.ds(0, 8)], r.hg1b.at[slot], r.hg1send.at[k], r.hg1recv.at[slot], prev_dev
                ).start()

            if k == 0:
                pl.when(begin * (1 - c) == 0)(send)
            else:
                send()

    def b1b():
        taps = [0.0, 0.0, 0.0]
        for k in range(CHUNKS):

            def get(k=k):
                await_bytes(r.hg1b.at[k], r.hg1recv.at[k])

            def zero(k=k):
                r.hg1b[k] = jnp.zeros((8, D), F32)

            if k == CHUNKS - 1:
                none = end * c
                pl.when(none == 0)(get)
                pl.when(none == 1)(zero)
            else:
                get()
            e = r.cv1.at[k]
            e[pl.ds(ROWS, 8)] = r.hg1b[k]
            gg = sum(r.trow[2 - j : 3 - j] * e[pl.ds(j, ROWS)] for j in range(3))
            rows = slice(k * ROWS, (k + 1) * ROWS)
            r.pbf1[rows, :D] = (gg * r.proj1[2, rows]).astype(BF)
            r.pbf1[rows, 2 * D :] = (gg * r.proj1[0, rows]).astype(BF)
            cvg = e[pl.ds(0, ROWS)]
            for j in range(3):
                taps[j] = taps[j] + jnp.sum(cvg * r.gp1[k, pl.ds(6 + j, ROWS)], 0, keepdims=True)
        r.tap1g[...] = jnp.concatenate(taps, 0)
        wide = dot_nn(r.pbf1[...], full_in())
        for k in (1, 0):
            rows = r.rg[1, k] + wide[k * ROWS : (k + 1) * ROWS]
            r.g0own[k] = rows
            u = r.gbf.at[k]
            u[z, y] = rows.astype(BF)
            ag_id["g", k] = ag_start(u)
            emit(1, k, rows, r.ligst, r.ig, 1)

    def b1_exchange():
        for k in range(CHUNKS):
            ag_id["r", 1, k] = ag_start(r.rb.at[1, k])
        for i in range(NW):
            lanes = slice(i * LW, (i + 1) * LW)
            for p in range(3):
                r.pms[i, :, p * LW : (p + 1) * LW] = r.pbf1[:, p * D + i * LW : p * D + (i + 1) * LW]
            r.pms[i, :, 3 * LW :] = r.mixed1[:, lanes]
        mine = r.pm.at[w]
        mine[...] = r.pms[w]

        def it(i, carry):
            dev = wa_peer(i)
            remote(r.pms.at[dev[2]], mine, r.pmsem.at[0], r.pmsem.at[1], dev).start()
            return carry

        lax.fori_loop(1, NW, it, 0)

    X = [r.Xgu, r.Xdn, r.Xcv]
    Y = [r.Ygu, r.Ydn, r.Ycv]
    R = [r.Rgu, r.Rdn, r.Rcv]
    flush = [
        [(r.Ygu, r.o_gu)],
        [(r.Ydn, r.o_dn)],
        [(r.Ycv.at[pl.ds(0, 3 * LW)], r.o_in), (r.Ycv.at[pl.ds(3 * LW, LW)], r.o_out)],
    ]

    def flush_copies(i):
        return [
            pltpu.make_async_copy(src, dst, r.lsem.at[len(loads) + i + n]) for n, (src, dst) in enumerate(flush[i])
        ]

    by_row = [True, False, True]

    def part(ref, i, q):
        if by_row[i]:
            size = ref.shape[0] // NX
            return ref.at[pl.ds(pl.multiple_of(q * size, size), size)]
        size = ref.shape[1] // NX
        return ref.at[:, pl.ds(pl.multiple_of(q * size, size), size)]

    def w1(l):
        for n0, n in tiles(D):
            cols = slice(n0, n0 + n)
            for g in range(2):
                r.Xgu[l, g * HW : (g + 1) * HW, cols] = sum(
                    dot_tn(r.gub[l, k, :, g * HP : (g + 1) * HP], flat(r.norm.at[l, k], cols))
                    for k in range(CHUNKS)
                )[:HW].astype(BF)
        for n0, n in tiles(D):
            r.Xdn[l, :, n0 : n0 + n] = sum(
                dot_tn(
                    r.hid[l, k],
                    outbf(l, k)[:, n0 : n0 + n] if l == 1 else flat(outbf(l, k), slice(n0, n0 + n)),
                )
                for k in range(CHUNKS)
            )[:HW].astype(BF)

    def w2_0():
        for n0, n in tiles(D):
            cols = slice(n0, n0 + n)
            r.Xcv[0, : 3 * LW, cols] = sum(
                dot_tn(r.pbf[k], r.tok[k, :, cols]) for k in range(CHUNKS)
            ).astype(BF)
            r.Xcv[0, 3 * LW :, cols] = sum(
                dot_tn(r.mixed[k], flat(r.rb.at[0, k], cols)) for k in range(CHUNKS)
            ).astype(BF)

    def w2_1():
        await_bytes(r.pm.at[pl.ds(0, NW - 1)], r.pmsem.at[1])
        for k in range(CHUNKS):
            ag_wait(ag_id["u", k], r.u1.at[k])
            ag_wait(ag_id["r", 1, k], r.rb.at[1, k])
        pm = [r.pm[:, k * ROWS : (k + 1) * ROWS].reshape(T, 4 * LW) for k in range(CHUNKS)]
        for n0, n in tiles(D):
            cols = slice(n0, n0 + n)
            r.Xcv[1, : 3 * LW, cols] = sum(
                dot_tn(pm[k][:, : 3 * LW], flat(r.u1.at[k], cols)) for k in range(CHUNKS)
            ).astype(BF)
            r.Xcv[1, 3 * LW :, cols] = sum(
                dot_tn(pm[k][:, 3 * LW :], flat(r.rb.at[1, k], cols)) for k in range(CHUNKS)
            ).astype(BF)

    def core_send(l, i):
        @pl.when(c != l)
        def _():
            remote(X[i].at[l], Y[i], r.csend.at[i], r.crecv.at[i], core_peer).start()

    def x_reduce(l, i):
        @pl.when(c == l)
        def _():
            await_bytes(Y[i], r.crecv.at[i])
            rows_total = Y[i].shape[0]

            def add(rows):
                X[i][l, rows] = (X[i][l, rows].astype(F32) + Y[i][rows].astype(F32)).astype(BF)

            row_loop(rows_total, 32, add)
            mine = R[i].at[x]
            for j in range(1, NX):
                dev = x_peer(j)
                remote(
                    part(X[i].at[l], i, dev[1]), mine, r.xsend.at[i], r.xrecv.at[i], dev
                ).start()

    def x_gather(l, i):
        @pl.when(c == l)
        def _():
            await_bytes(R[i].at[pl.ds(0, NX - 1)], r.xrecv.at[i])
            src = part(X[i].at[l], i, x)
            R[i][x] = src[...]
            dst = part(Y[i], i, x)
            rows_total = dst.shape[0]

            def add(rows):
                total = R[i][0, rows].astype(F32)
                for j in range(1, NX):
                    total = total + R[i][j, rows].astype(F32)
                dst[rows] = total.astype(BF)

            row_loop(rows_total, 16, add)
            for j in range(1, NX):
                remote(dst, dst, r.vsend.at[i], r.vrecv.at[i], x_peer(j)).start()

    def x_finish(l, i):
        @pl.when(c == l)
        def _():
            await_bytes(R[i].at[pl.ds(0, NX - 1)], r.vrecv.at[i])
            await_bytes(R[i].at[pl.ds(0, NX - 1)], r.xsend.at[i])
            await_bytes(R[i].at[pl.ds(0, NX - 1)], r.vsend.at[i])
            for cp in flush_copies(i):
                cp.start()

        @pl.when(c != l)
        def _():
            await_bytes(Y[i], r.csend.at[i])

    GR = D // 128

    def gain_send(l):
        st = r.gst.at[l]
        for i in range(GR):
            st[0, i : i + 1] = r.gacc[l, :, i * 128 : (i + 1) * 128]
        gain = st[0, 0:GR]
        for i in range(NW):
            st[i, 0:GR] = gain
            st[i, GR:] = jnp.zeros((8, 128), F32)
            if l == 1:
                st[i, GR : GR + 3, :LW] = r.tap1g[:, i * LW : (i + 1) * LW]
        mine = r.gex.at[l, w]
        mine[...] = st[w]

        def it(i, carry):
            dev = wa_peer(i)
            remote(st.at[dev[2]], mine, r.gsend.at[l], r.grecv.at[l], dev).start()
            return carry

        lax.fori_loop(1, NW, it, 0)

    def gain_recv(l):
        await_bytes(r.gex.at[l, pl.ds(0, NW - 1)], r.grecv.at[l])
        total = r.gex[l, 0]
        for i in range(1, NW):
            total = total + r.gex[l, i]
        r.sm[l] = total

    def small_send(l):
        if l == 0:
            r.sm[0, GR:] = r.sm[0, GR:] + r.tacc[...]

        @pl.when(c != l)
        def _():
            remote(r.sm.at[l], r.smY, r.csend.at[3], r.crecv.at[3], core_peer).start()

    def small_x(l):
        @pl.when(c == l)
        def _():
            await_bytes(r.smY, r.crecv.at[3])
            mine = r.smR.at[x]
            mine[...] = r.sm[l] + r.smY[...]
            for j in range(1, NX):
                remote(mine, mine, r.xsend.at[3], r.xrecv.at[3], x_peer(j)).start()

    def small_finish(l):
        @pl.when(c == l)
        def _():
            await_bytes(r.smR.at[pl.ds(0, NX - 1)], r.xrecv.at[3])
            total = r.smR[0]
            for j in range(1, NX):
                total = total + r.smR[j]
            for i in range(GR):
                r.o_gain[:, i * 128 : (i + 1) * 128] = total[i : i + 1]
            r.o_tap[...] = total[GR : GR + 3, :LW]
            await_bytes(r.smR.at[pl.ds(0, NX - 1)], r.xsend.at[3])

        @pl.when(c != l)
        def _():
            await_bytes(r.smY, r.csend.at[3])

    A, B = 0, 1
    AB, BA = (0, 1), (1, 0)
    s1(0, A)
    s1(0, B)
    gather_wa()
    s2(0, A)
    s2(0, B)
    gather_mid()
    mids("rs", 0, "a", AB)
    gather_x(0)
    s3(0, A)
    s3(0, B)
    gather_x(1)
    mids("ag", 0, "n", AB)
    s4(0, A)
    s4_down(0, A)
    s4(0, B)
    s4_down(0, B)
    gather_x(2)
    prep_cot(A)
    mids("rs", 0, "b", AB)
    gather_core(0)
    gather_x(3)
    prep_cot(B)
    s5(0, A)
    s5(0, B)
    gather_core(1)
    f1a()
    gather_core(3)
    f1b()
    mids("ag", 1, "n", AB)
    u_start()
    s4(1, A)
    s4(1, B)
    t1(1, B)
    t1(1, A)
    mids("rs", 1, "c", BA)
    w1(1)
    t2(1, B)
    t2(1, A)
    mids("ag", 1, "u", AB)
    b1a()
    s4_down(1, A)
    s4_down(1, B)
    core_send(1, 0)
    core_send(1, 1)
    b1b()
    mids("ag", 0, "g", BA)
    gain_send(1)
    mids("rs", 1, "b", AB)
    b1_exchange()
    x_reduce(1, 0)
    x_reduce(1, 1)
    t1(0, B)
    t1(0, A)
    w1(0)
    core_send(0, 0)
    core_send(0, 1)
    s5(1, A)
    s5(1, B)
    mids("rs", 0, "c", BA)
    mids("ag", 1, "r", BA)
    gain_recv(1)
    small_send(1)
    x_gather(1, 0)
    x_gather(1, 1)
    x_reduce(0, 0)
    x_reduce(0, 1)
    t2(0, B)
    t2(0, A)
    mids("ag", 0, "r", BA)
    gain_send(0)
    w2_1()
    core_send(1, 2)
    t3(0, B)
    t3(0, A)
    x_reduce(1, 2)
    small_x(1)
    x_gather(0, 0)
    x_gather(0, 1)
    t4(0, B)
    t4(0, A)
    w2_0()
    core_send(0, 2)
    mids("rs", 0, "d", BA)
    x_reduce(0, 2)
    gain_recv(0)
    small_send(0)
    small_x(0)
    x_gather(1, 2)
    t5(0, B)
    t5(0, A)
    for i in range(3):
        x_finish(1, i)
    x_gather(0, 2)
    small_finish(1)
    for i in range(3):
        x_finish(0, i)
    small_finish(0)
    gather_close()
    await_bytes(r.pm.at[pl.ds(0, NW - 1)], r.pmsem.at[0])

    for sems, staging, target, out in ((0, r.lost, r.lo, r.o_layer), (1, r.ligst, r.ig, r.o_grad)):
        for k in range(CHUNKS):
            await_bytes(staging.at[0, k], r.orecv.at[sems, k])
            await_bytes(staging.at[0, k], r.osend.at[sems, k])
        out[...] = target[...]
    for n, buf in ag_sent:
        for i in range(2):
            await_bytes(ag_first(buf), r.ags.at[n, i])
            await_bytes(ag_second(buf), r.ags.at[n, 2 + i])
    for uses in stage_use:
        for n, buf in uses[-2:]:
            stage_sent(n, buf)
        for n, buf in uses:
            await_bytes(r.rwa.at[n, pl.ds(0, NZ - 1)], r.rss.at[n, 2])
            await_bytes(r.rwb.at[n, pl.ds(0, NY - 1)], r.rss.at[n, 3])
    for l in range(2):
        await_bytes(r.gex.at[l, pl.ds(0, NW - 1)], r.gsend.at[l])
    for fsem, fbuf, bsem, bbuf, no_next, no_prev in (
        (r.hsend, r.hs, r.hgsend, r.hgs, last * c, first * (1 - c)),
        (r.h1send, r.h1s, r.hg1send, r.hg1b, end * c, begin * (1 - c)),
    ):
        for k in range(CHUNKS):

            def fwd(k=k, fsem=fsem, fbuf=fbuf):
                await_bytes(fbuf.at[k], fsem.at[k])

            def bwd(k=k, bsem=bsem, bbuf=bbuf):
                await_bytes(bbuf.at[k], bsem.at[k])

            if k == CHUNKS - 1:
                pl.when(no_next == 0)(fwd)
            else:
                fwd()
            if k == 0:
                pl.when(no_prev == 0)(bwd)
            else:
                bwd()
    for cp in wcopies:
        cp.wait_send()
    for i in range(3):
        for cp in flush_copies(i):
            cp.wait()


def body(NX, NW, tokens, cotangent, in_weight, conv_weight, out_weight, norm_gain, gate_up_weight, down_weight):
    micro, T, D = tokens.shape
    LW = conv_weight.shape[2]
    HW = gate_up_weight.shape[3]
    HP = -(-HW // 128) * 128
    GR = D // 128
    L, K = 2, CHUNKS
    vmem = pltpu.VMEM
    dma = pltpu.SemaphoreType.DMA
    n_ag, n_rs = 6 * K, 6 * K
    NY = NZ = next(i for i in range(1, NW + 1) if i * i >= NW)
    plane = (NZ, NY, ROWS, D)
    ins = dict(
        tokens=tokens, cotangent=cotangent, w_in=in_weight[0].transpose(1, 2, 0), w_out=out_weight[0],
        w_gu=gate_up_weight[0].transpose(1, 2, 0), w_dn=down_weight[0],
        w_gain=norm_gain, w_conv=conv_weight.transpose(1, 0, 2)
    )
    anyspec = pl.BlockSpec(memory_space=pl.ANY)
    vspec = pl.BlockSpec(memory_space=pltpu.VMEM)
    shape = jax.ShapeDtypeStruct
    outs = dict(
        o_layer=(shape((micro, ROWS, D), BF), vspec),
        o_grad=(shape((micro, ROWS, D), F32), vspec),
        o_in=(shape((3 * LW, D), BF), anyspec),
        o_out=(shape((LW, D), BF), anyspec),
        o_gu=(shape((2 * HW, D), BF), anyspec),
        o_dn=(shape((HW, D), BF), anyspec),
        o_gain=(shape((1, D), F32), vspec),
        o_tap=(shape((3, LW), F32), vspec),
    )
    scratch = dict(
        Cown=vmem((L, 4, LW, D), BF), Cfull=vmem((4, NZ, NY, LW, D), BF),
        Wgu=vmem((L, 2, HP, D), BF), Wdn=vmem((L, HP, D), BF), Wsm=vmem((L, 8, D), F32),
        tok=vmem((K, T, D), BF), cot=vmem((K, T, D), F32), cotb=vmem((K, T, D), BF),
        projB=vmem((K, T, LW), F32), projC=vmem((K, T, LW), F32), projX=vmem((K, T, LW), F32),
        gp=vmem((K, T + 8, LW), F32), conv=vmem((K, T, LW), F32), mixed=vmem((K, T, LW), BF),
        gu=vmem((L, K, T, 2 * HP), F32), hg=vmem((K, T, HP), F32), hid=vmem((L, K, T, HP), BF),
        gub=vmem((L, K, T, 2 * HP), BF), pbf=vmem((K, T, 3 * LW), BF),
        res=vmem((L, K, ROWS, D), F32), rg=vmem((L, K, ROWS, D), F32), g0own=vmem((K, ROWS, D), F32),
        cvg=vmem((K, T + 8, LW), F32),
        norm=vmem((L, K) + plane, BF), u1=vmem((K,) + plane, BF), rb=vmem((L, K) + plane, BF), gbf=vmem((K,) + plane, BF),
        stage=vmem((K, 2) + plane, BF), rva=vmem((n_rs, NY, NZ, ROWS, D // 2), BF), rvb=vmem((n_rs, NZ, NY, ROWS, D // 2), BF),
        rsa=vmem((n_rs, NZ, ROWS, D // 2), BF), rsb=vmem((n_rs, NY, ROWS, D // 2), BF),
        rwa=vmem((n_rs, NZ, ROWS, D // 2), BF), rwb=vmem((n_rs, NY, ROWS, D // 2), BF),
        hs=vmem((K, 16, LW), BF), hb=vmem((K, 16, LW), BF), hgs=vmem((K, 8, LW), F32), hgb=vmem((K, 8, LW), F32),
        proj1=vmem((3, K * ROWS, D), F32), gp1=vmem((K, ROWS + 8, D), F32), conv1=vmem((K, ROWS, D), F32),
        mixed1=vmem((K * ROWS, D), BF), cv1=vmem((K, ROWS + 8, D), F32), pbf1=vmem((K * ROWS, 3 * D), BF),
        h1s=vmem((K, ROWS, D), BF), h1b=vmem((K, ROWS, D), BF), hg1b=vmem((K, 8, D), F32),
        trow=vmem((3, D), F32), tap1g=vmem((3, D), F32), taps1=vmem((NW, 8, 128), F32),
        pms=vmem((NW, K * ROWS, 4 * LW), BF), pm=vmem((NW, K * ROWS, 4 * LW), BF),
        lost=vmem((L, K, ROWS, D), BF), ligst=vmem((L, K, ROWS, D), F32),
        lo=vmem((micro, ROWS, D), BF), ig=vmem((micro, ROWS, D), F32),
        Xgu=vmem((L, 2 * HW, D), BF), Xdn=vmem((L, HW, D), BF), Xcv=vmem((L, 4 * LW, D), BF),
        Ygu=vmem((2 * HW, D), BF), Ydn=vmem((HW, D), BF), Ycv=vmem((4 * LW, D), BF),
        Rgu=vmem((NX, 2 * HW // NX, D), BF), Rdn=vmem((NX, HW, D // NX), BF), Rcv=vmem((NX, 4 * LW // NX, D), BF),
        gacc=vmem((L, 1, D), F32), tacc=vmem((8, 128), F32), gst=vmem((L, NW, GR + 8, 128), F32),
        gex=vmem((L, NW, GR + 8, 128), F32), sm=vmem((L, GR + 8, 128), F32),
        smY=vmem((GR + 8, 128), F32), smR=vmem((NX, GR + 8, 128), F32),
        lsem=dma((16,)), wsend=dma((5,)), wrecv=dma((5,)), ags=dma((n_ag, 4)), agr=dma((n_ag, 4)),
        rss=dma((n_rs, 4)), rsr=dma((n_rs, 4)), hsend=dma((K,)), hrecv=dma((K,)), hgsend=dma((K,)), hgrecv=dma((K,)),
        h1send=dma((K,)), h1recv=dma((K,)), hg1send=dma((K,)), hg1recv=dma((K,)), pmsem=dma((2,)),
        gwsem=dma((11,)), gxs=dma((4,)), gxr=dma((4,)), gcs=dma((4,)), gcr=dma((4,)),
        osend=dma((2, K)), orecv=dma((2, K)), csend=dma((4,)), crecv=dma((4,)), xsend=dma((4,)), xrecv=dma((4,)),
        vsend=dma((3,)), vrecv=dma((3,)), gsend=dma((L,)), grecv=dma((L,)),
    )
    names = tuple(ins) + tuple(outs) + tuple(scratch)
    layer, grad, g_in, g_out, g_gu, g_dn, g_gain, g_tap = pl.pallas_call(
        functools.partial(kernel, (NX, NW, T, D, LW, HW, HP), names),
        out_shape=tuple(o[0] for o in outs.values()),
        in_specs=[anyspec] * (len(ins) - 2) + [vspec] * 2,
        out_specs=tuple(o[1] for o in outs.values()),
        scratch_shapes=list(scratch.values()),
        compiler_params=pltpu.CompilerParams(
            collective_id=0, has_side_effects=True, vmem_limit_bytes=63 << 20
        ),
    )(*ins.values())
    return (
        layer[None],
        grad[None],
        g_in.reshape(3, LW, D).transpose(2, 0, 1).astype(F32)[None],
        g_tap[None],
        g_out.astype(F32)[None],
        g_gain,
        g_gu.reshape(2, HW, D).transpose(2, 0, 1).astype(F32)[None],
        g_dn.astype(F32)[None],
    )


def solution(mesh):
    in_specs = (
        P(None, "seq", None),
        P(None, "seq", None),
        P("section", None, None, "wa"),
        P("section", None, "wa"),
        P("section", "wa", None),
        P("section", None),
        P("section", None, None, "wa"),
        P("section", "wa", None),
    )
    out_specs = (
        P("section", None, ("seq", "wa"), None),
        P("section", None, ("seq", "wa"), None),
        P("section", None, None, "wa"),
        P("section", None, "wa"),
        P("section", "wa", None),
        P("section", None),
        P("section", None, None, "wa"),
        P("section", "wa", None),
    )
    fn = functools.partial(body, mesh.shape["seq"], mesh.shape["wa"])
    return jax.shard_map(fn, mesh=mesh, in_specs=in_specs, out_specs=out_specs, check_vma=False)
```

```python
import functools
import types

import jax
import jax.numpy as jnp
from jax import lax
from jax.experimental import pallas as pl
from jax.experimental.pallas import tpu as pltpu
from jax.sharding import PartitionSpec as P

EPSILON = 1e-05
MESH = pl.DeviceIdType.MESH
BF = jnp.bfloat16
F32 = jnp.float32
ROWS = 16
CHUNKS = 2


def dot_nn(a, b):
    return jnp.dot(a, b, preferred_element_type=F32)


def dot_nt(a, b):
    return lax.dot_general(a, b, (((1,), (1,)), ((), ())), preferred_element_type=F32)


def dot_tn(a, b):
    return lax.dot_general(a, b, (((0,), (0,)), ((), ())), preferred_element_type=F32)


def tiles(total, size=256):
    return [(start, min(size, total - start)) for start in range(0, total, size)]


def row_loop(total, step, fn):
    def it(i, carry):
        fn(pl.ds(pl.multiple_of(i * step, step), step))
        return carry

    lax.fori_loop(0, total // step, it, 0)


def kernel(cfg, names, *refs):
    NX, NW, T, D, LW, HW, HP = cfg
    r = types.SimpleNamespace(**dict(zip(names, refs, strict=True)))
    c = lax.axis_index("section")
    x = lax.axis_index("seq")
    w = lax.axis_index("wa")
    last = (x + 1) // NX
    first = (NX - x) // NX
    own = pl.ds(pl.multiple_of(w * ROWS, ROWS), ROWS)
    core_peer = (1 - c, x, w)
    NY = NZ = next(i for i in range(1, NW + 1) if i * i >= NW)
    z = w // NY
    y = w - z * NY
    LO, HI = pl.ds(0, D // 2), pl.ds(D // 2, D // 2)
    w_last = (w + 1) // NW
    w_first = (NW - w) // NW
    end = last * w_last
    begin = first * w_first
    next_dev = (c + end * (1 - 2 * c), lax.rem(x + w_last, NX), lax.rem(w + 1, NW))
    prev_dev = (c + begin * (1 - 2 * c), lax.rem(x + NX - w_first, NX), lax.rem(w + NW - 1, NW))

    def y_at(i):
        return lax.rem(y + i, NY)

    def z_at(i):
        return lax.rem(z + i, NZ)

    def y_peer(i):
        return (c, x, z * NY + y_at(i))

    def z_peer(i):
        return (c, x, z_at(i) * NY + y)

    def flat(ref, *cols):
        value = ref[(slice(None),) * 3 + cols] if cols else ref[...]
        return value.reshape(T, value.shape[-1])

    def wa_peer(i):
        return (c, x, lax.rem(w + i, NW))

    def x_peer(i):
        return (c, lax.rem(x + i, NX), w)

    def remote(src, dst, send, recv, dev):
        return pltpu.make_async_remote_copy(
            src_ref=src, dst_ref=dst, send_sem=send, recv_sem=recv, device_id=dev, device_id_type=MESH
        )

    def await_bytes(ref, sem):
        pltpu.make_async_copy(ref, ref, sem).wait()

    loads = []

    def load(src, dst):
        cp = pltpu.make_async_copy(src, dst, r.lsem.at[len(loads)])
        cp.start()
        loads.append(cp)
        return len(loads) - 1

    wpairs = [
        (r.w_in, r.Cown.at[c, pl.ds(0, 3)]),
        (r.Wsm.at[c], r.Wsm.at[c]),
        (r.w_gu, r.Wgu.at[c, :, pl.ds(0, HW)]),
        (r.w_dn, r.Wdn.at[c, pl.ds(0, HW)]),
        (r.w_out, r.Cown.at[c, 3]),
    ]
    l_tok = [load(r.tokens.at[c], r.tok.at[0]), None]
    l_w = [load(*wpairs[0]), None]
    l_tok[1] = load(r.tokens.at[2 + c], r.tok.at[1])
    l_w += [load(*p) for p in wpairs[2:]]
    l_cot = [load(r.cotangent.at[2 * k + c], r.cot.at[k]) for k in range(CHUNKS)]

    r.Wsm[c] = jnp.zeros((8, D), F32)
    r.Wsm[c, 0:1] = r.w_gain[...]
    for j in range(3):
        r.Wsm[c, j + 1 : j + 2, :LW] = r.w_conv[j]

    bar = pltpu.get_barrier_semaphore()

    def sig(dev):
        pl.semaphore_signal(bar, inc=1, device_id=dev, device_id_type=MESH)

    sig(core_peer)

    def sig_wa(i, carry):
        sig(wa_peer(i))
        return carry

    lax.fori_loop(1, NW, sig_wa, 0)
    for i in range(1, NX):
        sig(x_peer(i))
    sig((1 - c, lax.rem(x + 1, NX), w))
    sig((1 - c, lax.rem(x + NX - 1, NX), w))
    sig(next_dev)
    sig(prev_dev)
    if HP > HW:
        for l in range(2):
            r.Wdn[l, HW:] = jnp.zeros((HP - HW, D), BF)
            r.Wgu[l, :, HW:] = jnp.zeros((2, HP - HW, D), BF)
    r.gacc[...] = jnp.zeros(r.gacc.shape, F32)
    r.tacc[...] = jnp.zeros(r.tacc.shape, F32)
    pl.semaphore_wait(bar, (NW - 1) + (NX - 1) + 5)

    wcopies = []
    for i, (src, dst) in enumerate(wpairs):
        cp = remote(src, dst, r.wsend.at[i], r.wrecv.at[i], core_peer)
        cp.start()
        wcopies.append(cp)
    wready = set()

    def need_w(i):
        if i not in wready:
            wready.add(i)
            if l_w[i] is not None:
                loads[l_w[i]].wait()
            wcopies[i].wait_recv()

    full = r.Cfull
    HALF = D // 2
    LQ = LW // NX
    xrows = pl.ds(pl.multiple_of(x * LQ, LQ), LQ)
    clanes = pl.ds(pl.multiple_of(c * HALF, HALF), HALF)
    la, lb = (pl.ds(pl.multiple_of(c * HALF + h, HALF // 2), HALF // 2) for h in (0, HALF // 2))
    first_a, first_b = full.at[:, 0, 0 : NY - 1, xrows, la], full.at[:, 0 : NZ - 1, 0, xrows, lb]
    second_a, second_b = full.at[:, 0 : NZ - 1, :, xrows, la], full.at[:, :, 0 : NY - 1, xrows, lb]

    def gather_wa():
        need_w(0)
        need_w(1)
        need_w(4)
        local = pltpu.make_async_copy(
            r.Cown.at[1, :, xrows, clanes], full.at[:, z, y, xrows, clanes], r.gwsem.at[0]
        )
        local.start()
        for lanes, peer, count, sem in ((la, y_peer, NY, 1), (lb, z_peer, NZ, 5)):
            for i in range(1, count):
                remote(
                    r.Cown.at[1, :, xrows, lanes], full.at[:, z, y, xrows, lanes],
                    r.gwsem.at[sem], r.gwsem.at[sem + 1], peer(i),
                ).start()
        tap = r.Wsm.at[1, :, pl.ds(0, 128)]
        tap_dst = r.taps1.at[w]
        tap_dst[...] = tap[...]

        def it(i, carry):
            remote(tap, tap_dst, r.gwsem.at[3], r.gwsem.at[4], wa_peer(i)).start()
            return carry

        lax.fori_loop(1, NW, it, 0)
        local.wait()

    def gather_mid():
        await_bytes(first_a, r.gwsem.at[2])
        piece = full.at[:, z, :, xrows, la]
        for i in range(1, NZ):
            remote(piece, piece, r.gwsem.at[7], r.gwsem.at[8], z_peer(i)).start()
        await_bytes(first_b, r.gwsem.at[6])
        piece = full.at[:, :, y, xrows, lb]
        for i in range(1, NY):
            remote(piece, piece, r.gwsem.at[9], r.gwsem.at[10], y_peer(i)).start()

    def gather_x(p):
        if p == 0:
            await_bytes(second_a, r.gwsem.at[8])
            await_bytes(second_b, r.gwsem.at[10])
        piece = full.at[p, :, :, xrows, clanes]
        for j in range(1, NX):
            remote(piece, piece, r.gxs.at[p], r.gxr.at[p], x_peer(j)).start()

    def gather_core(p):
        await_bytes(full.at[p, :, :, pl.ds(0, (NX - 1) * LQ), clanes], r.gxr.at[p])
        piece = full.at[p, :, :, :, clanes]
        remote(piece, piece, r.gcs.at[p], r.gcr.at[p], core_peer).start()

    def gather_done(p):
        await_bytes(full.at[p, :, :, :, clanes], r.gcr.at[p])

    def gather_close():
        for ref, sem in ((first_a, 1), (first_b, 5), (second_a, 7), (second_b, 9)):
            await_bytes(ref, r.gwsem.at[sem])
        await_bytes(r.taps1.at[pl.ds(0, NW - 1)], r.gwsem.at[3])
        for p in range(4):
            await_bytes(full.at[p, :, :, pl.ds(0, (NX - 1) * LQ), clanes], r.gxs.at[p])
            await_bytes(full.at[p, :, :, :, clanes], r.gcs.at[p])

    counts = {"ag": 0, "rs": 0}
    ag_sent, rs_sent = [], []

    def ag_start(buf):
        n = counts["ag"]
        counts["ag"] += 1
        lo, hi = buf.at[z, y, :, LO], buf.at[z, y, :, HI]
        for i in range(1, NY):
            remote(lo, lo, r.ags.at[n, 0], r.agr.at[n, 0], y_peer(i)).start()
            remote(hi, hi, r.ags.at[n, 1], r.agr.at[n, 1], z_peer(i)).start()
        ag_sent.append((n, buf))
        return n

    def ag_first(buf):
        return buf.at[0, pl.ds(0, NY - 1), :, LO]

    def ag_second(buf):
        return buf.at[pl.ds(0, NZ - 1), :, :, LO]

    def ag_mid(n, buf):
        lo, hi = buf.at[z, :, :, LO], buf.at[:, y, :, HI]
        await_bytes(ag_first(buf), r.agr.at[n, 0])
        for i in range(1, NZ):
            remote(lo, lo, r.ags.at[n, 2], r.agr.at[n, 2], z_peer(i)).start()
        await_bytes(ag_first(buf), r.agr.at[n, 1])
        for i in range(1, NY):
            remote(hi, hi, r.ags.at[n, 3], r.agr.at[n, 3], y_peer(i)).start()

    def ag_wait(n, buf):
        for i in (2, 3):
            await_bytes(ag_second(buf), r.agr.at[n, i])

    stage_use = [[], []]

    def stage_get(k):
        uses = stage_use[k]
        slot = len(uses) % 2
        if len(uses) >= 2:
            stage_sent(*uses[-2])
        return r.stage.at[k, slot]

    def stage_sent(n, buf):
        for i in (0, 1):
            await_bytes(ag_second(buf), r.rss.at[n, i])

    def rs_start(k, buf):
        n = counts["rs"]
        counts["rs"] += 1
        for i in range(1, NY):
            remote(
                buf.at[:, y_at(i), :, LO], r.rva.at[n, y], r.rss.at[n, 0], r.rsr.at[n, 0], y_peer(i)
            ).start()
            remote(
                buf.at[z_at(i), :, :, HI], r.rvb.at[n, z], r.rss.at[n, 1], r.rsr.at[n, 1], z_peer(i)
            ).start()
        stage_use[k].append((n, buf))
        return n

    def rs_mid(n, k):
        buf = dict(stage_use[k])[n]
        sa, sb = r.rsa.at[n], r.rsb.at[n]
        await_bytes(r.rva.at[n, pl.ds(0, NY - 1)], r.rsr.at[n, 0])
        total = buf[:, y, :, LO].astype(F32)
        for i in range(1, NY):
            total = total + r.rva[n, y_at(i)].astype(F32)
        sa[...] = total.astype(BF)
        for i in range(1, NZ):
            remote(sa.at[z_at(i)], r.rwa.at[n, z], r.rss.at[n, 2], r.rsr.at[n, 2], z_peer(i)).start()
        await_bytes(r.rvb.at[n, pl.ds(0, NZ - 1)], r.rsr.at[n, 1])
        total = buf[z, :, :, HI].astype(F32)
        for i in range(1, NZ):
            total = total + r.rvb[n, z_at(i)].astype(F32)
        sb[...] = total.astype(BF)
        for i in range(1, NY):
            remote(sb.at[y_at(i)], r.rwb.at[n, y], r.rss.at[n, 3], r.rsr.at[n, 3], y_peer(i)).start()

    def rs_sum(n):
        await_bytes(r.rwa.at[n, pl.ds(0, NZ - 1)], r.rsr.at[n, 2])
        lo = r.rsa[n, z].astype(F32)
        for i in range(1, NZ):
            lo = lo + r.rwa[n, z_at(i)].astype(F32)
        await_bytes(r.rwb.at[n, pl.ds(0, NY - 1)], r.rsr.at[n, 3])
        hi = r.rsb[n, y].astype(F32)
        for i in range(1, NY):
            hi = hi + r.rwb[n, y_at(i)].astype(F32)
        return jnp.concatenate([lo, hi], 1)

    def mids(kind, l, name, ks):
        for k in ks:
            if kind == "rs":
                rs_mid(rs_id[name, l, k], k)
            else:
                key, buf = {
                    "n": (("n", l, k), r.norm.at[l, k]),
                    "u": (("u", k), r.u1.at[k]),
                    "r": (("r", l, k), r.rb.at[l, k]),
                    "g": (("g", k), r.gbf.at[k]),
                }[name]
                ag_mid(ag_id[key], buf)

    rs_id, ag_id = {}, {}

    def u_of(l, k):
        return r.tok.at[k] if l == 0 else r.u1.at[k]

    hcopy = {}

    w0 = r.Cown.at[0]

    def put(ref, n0, n, value):
        ref[:, :, :, n0 : n0 + n] = value.astype(BF).reshape(NZ, NY, ROWS, n)

    def s1(l, k):
        u = u_of(l, k)
        loads[l_tok[k]].wait()
        need_w(0)
        projected = dot_nt(u[...], w0[0:3].reshape(3 * LW, D))
        b_part = projected[:, :LW]
        x_part = projected[:, 2 * LW :]
        r.projB[k] = b_part
        r.projC[k] = projected[:, LW : 2 * LW]
        r.projX[k] = x_part
        gated = (b_part * x_part).astype(BF)
        r.gp[k, pl.ds(8, T)] = gated.astype(F32)
        r.hs[k] = gated[T - 16 :]

        slot = k + last * c

        def send():
            remote(
                r.hs.at[k],
                r.hb.at[slot],
                r.hsend.at[k],
                r.hrecv.at[slot],
                (c + last * (1 - 2 * c), lax.rem(x + 1, NX), w),
            ).start()

        if k == CHUNKS - 1:
            pl.when(last * c == 0)(send)
        else:
            send()

    def s2(l, k):
        def get():
            await_bytes(r.hb.at[k], r.hrecv.at[k])

        def zero():
            r.hb[k] = jnp.zeros((16, LW), BF)

        if k == 0:
            none = first * (1 - c)
            pl.when(none == 0)(get)
            pl.when(none == 1)(zero)
        else:
            get()
        need_w(1)
        need_w(4)
        r.gp[k, pl.ds(0, 8)] = r.hb[k].astype(F32)[8:]
        taps = r.Wsm[l]
        conv = (
            taps[1:2, :LW] * r.gp[k, pl.ds(6, T)]
            + taps[2:3, :LW] * r.gp[k, pl.ds(7, T)]
            + taps[3:4, :LW] * r.gp[k, pl.ds(8, T)]
        )
        r.conv[k] = conv
        r.mixed[k] = (r.projC[k] * conv).astype(BF)
        buf = stage_get(k)
        for n0, n in tiles(D):
            put(buf, n0, n, dot_nn(r.mixed[k], w0[3, :, n0 : n0 + n]))
        rs_id["a", l, k] = rs_start(k, buf)

    def inv_rms(res):
        return lax.rsqrt(jnp.mean(res * res, -1, keepdims=True) + EPSILON)

    def s3(l, k):
        res = r.tok[k, own].astype(F32) + rs_sum(rs_id["a", l, k])
        r.res[l, k] = res
        buf = r.norm.at[l, k]
        buf[z, y] = (res * inv_rms(res) * r.Wsm[l, 0:1]).astype(BF)
        ag_id["n", l, k] = ag_start(buf)

    def s4(l, k):
        buf = r.norm.at[l, k]
        ag_wait(ag_id["n", l, k], buf)
        need_w(2)
        need_w(3)
        gu = r.gu.at[l, k]
        for g in range(2):
            gu[:, g * HP : (g + 1) * HP] = dot_nt(flat(buf), r.Wgu[l, g])

        def act(rows):
            gate = gu[rows, :HP]
            up = gu[rows, HP:]
            r.hid[l, k, rows] = (gate * jax.nn.sigmoid(gate) * up).astype(BF)

        row_loop(T, 32, act)

    def s4_down(l, k):
        st = stage_get(k)
        for n0, n in tiles(D):
            put(st, n0, n, dot_nn(r.hid[l, k], r.Wdn[l, :, n0 : n0 + n]))
        rs_id["b", l, k] = rs_start(k, st)

    def emit(l, k, value, staging, target, sems):
        staging[l, k] = value

        @pl.when(c == l)
        def _():
            target[2 * k + c] = value

        @pl.when(c != l)
        def _():
            remote(
                staging.at[l, k],
                target.at[2 * k + c],
                r.osend.at[sems, k],
                r.orecv.at[sems, k],
                core_peer,
            ).start()

    def s5(l, k):
        rows = (r.res[l, k] + rs_sum(rs_id["b", l, k])).astype(BF)
        if l == 0:
            r.u1[k, z, y] = rows
        emit(l, k, rows, r.lost, r.lo, 0)

    def outbf(l, k):
        return r.cotb.at[k] if l == 1 else r.gbf.at[k]

    def prep_cot(k):
        loads[l_cot[k]].wait()

        def cast(rows):
            r.cotb[k, rows] = r.cot[k, rows].astype(BF)

        row_loop(T, 32, cast)

    def t1(l, k):
        ob = outbf(l, k)
        if l == 0:
            ag_wait(ag_id["g", k], ob)
        hg = r.hg.at[k]
        for n0, n in tiles(HP):
            hg[:, n0 : n0 + n] = dot_nt(ob[...] if l == 1 else flat(ob), r.Wdn[l, n0 : n0 + n])
        gu = r.gu.at[l, k]
        gub = r.gub.at[l, k]

        def act(rows):
            gate = gu[rows, :HP]
            up = gu[rows, HP:]
            h = hg[rows]
            s = jax.nn.sigmoid(gate)
            gub[rows, :HP] = (h * up * (s * (1.0 + gate * (1.0 - s)))).astype(BF)
            gub[rows, HP:] = (h * (gate * s)).astype(BF)

        row_loop(T, 32, act)
        st = stage_get(k)
        for n0, n in tiles(D):
            put(st, n0, n, dot_nn(gub[...], r.Wgu[l, :, :, n0 : n0 + n].reshape(2 * HP, n)))
        rs_id["c", l, k] = rs_start(k, st)

    def t2(l, k):
        ng = rs_sum(rs_id["c", l, k])
        res = r.res[l, k]
        inv = inv_rms(res)
        g = r.cot[k, own] if l == 1 else r.g0own[k]
        r.gacc[l] = r.gacc[l] + jnp.sum(ng * res * inv, 0, keepdims=True)
        scaled = ng * r.Wsm[l, 0:1]
        rg = g + inv * scaled - res * (inv * inv * inv) * jnp.mean(scaled * res, -1, keepdims=True)
        r.rg[l, k] = rg
        buf = r.rb.at[l, k]
        buf[z, y] = rg.astype(BF)
        if l == 0:
            ag_id["r", l, k] = ag_start(buf)

    def t3(l, k):
        buf = r.rb.at[l, k]
        ag_wait(ag_id["r", l, k], buf)
        mg = dot_nt(flat(buf), w0[3])
        r.pbf[k, :, LW : 2 * LW] = (mg * r.conv[k]).astype(BF)
        cvg = mg * r.projC[k]
        r.cvg[k, pl.ds(0, T)] = cvg
        r.hgs[k] = cvg[:8]
        slot = k - first * (1 - c)

        def send():
            remote(
                r.hgs.at[k],
                r.hgb.at[slot],
                r.hgsend.at[k],
                r.hgrecv.at[slot],
                (c + first * (1 - 2 * c), lax.rem(x + NX - 1, NX), w),
            ).start()

        if k == 0:
            pl.when(first * (1 - c) == 0)(send)
        else:
            send()

    def t4(l, k):
        def get():
            await_bytes(r.hgb.at[k], r.hgrecv.at[k])

        def zero():
            r.hgb[k] = jnp.zeros((8, LW), F32)

        if k == CHUNKS - 1:
            none = last * c
            pl.when(none == 0)(get)
            pl.when(none == 1)(zero)
        else:
            get()
        e = r.cvg.at[k]
        e[pl.ds(T, 8)] = r.hgb[k]
        taps = r.Wsm[l]
        gg = (
            taps[3:4, :LW] * e[pl.ds(0, T)]
            + taps[2:3, :LW] * e[pl.ds(1, T)]
            + taps[1:2, :LW] * e[pl.ds(2, T)]
        )
        pbf = r.pbf.at[k]
        pbf[:, :LW] = (gg * r.projX[k]).astype(BF)
        pbf[:, 2 * LW :] = (gg * r.projB[k]).astype(BF)
        st = stage_get(k)
        for n0, n in tiles(D):
            put(st, n0, n, dot_nn(pbf[...], w0[0:3, :, n0 : n0 + n].reshape(3 * LW, n)))
        rs_id["d", l, k] = rs_start(k, st)
        cvg = e[pl.ds(0, T)]
        for j in range(3):
            r.tacc[j : j + 1, :LW] = r.tacc[j : j + 1, :LW] + jnp.sum(
                cvg * r.gp[k, pl.ds(6 + j, T)], 0, keepdims=True
            )

    def t5(l, k):
        rows = r.rg[l, k] + rs_sum(rs_id["d", l, k])
        emit(l, k, rows, r.ligst, r.ig, 1)

    def full_in():
        return full[0:3].reshape(3 * D, D)

    def taps_row(j):
        return jnp.concatenate([r.taps1[i, j : j + 1, :LW] for i in range(NW)], 1)

    def f1a():
        u = jnp.concatenate([r.u1[k, z, y] for k in range(CHUNKS)], 0)
        for p in range(3):
            gather_done(p)
            if p == 1:
                gather_core(2)
            r.proj1[p] = dot_nt(u, full[p].reshape(D, D))
        gated = (r.proj1[0] * r.proj1[2]).astype(BF)
        for k in range(CHUNKS):
            g = gated[k * ROWS : (k + 1) * ROWS]
            r.gp1[k, pl.ds(8, ROWS)] = g.astype(F32)
            r.h1s[k] = g
            slot = k + end * c

            def send(k=k, slot=slot):
                remote(
                    r.h1s.at[k], r.h1b.at[slot], r.h1send.at[k], r.h1recv.at[slot], next_dev
                ).start()

            if k == CHUNKS - 1:
                pl.when(end * c == 0)(send)
            else:
                send()

    def f1b():
        await_bytes(r.taps1.at[pl.ds(0, NW - 1)], r.gwsem.at[4])
        r.trow[...] = jnp.concatenate([taps_row(j + 1) for j in range(3)], 0)
        for k in range(CHUNKS):

            def get(k=k):
                await_bytes(r.h1b.at[k], r.h1recv.at[k])

            def zero(k=k):
                r.h1b[k] = jnp.zeros((ROWS, D), BF)

            if k == 0:
                none = begin * (1 - c)
                pl.when(none == 0)(get)
                pl.when(none == 1)(zero)
            else:
                get()
            r.gp1[k, pl.ds(0, 8)] = r.h1b[k].astype(F32)[8:]
            conv = sum(r.trow[j : j + 1] * r.gp1[k, pl.ds(6 + j, ROWS)] for j in range(3))
            r.conv1[k] = conv
            rows = slice(k * ROWS, (k + 1) * ROWS)
            r.mixed1[rows] = (r.proj1[1, rows] * conv).astype(BF)
        gather_done(3)
        wide = dot_nn(r.mixed1[...], full[3].reshape(D, D))
        for k in range(CHUNKS):
            res = r.u1[k, z, y].astype(F32) + wide[k * ROWS : (k + 1) * ROWS]
            r.res[1, k] = res
            buf = r.norm.at[1, k]
            buf[z, y] = (res * inv_rms(res) * r.Wsm[1, 0:1]).astype(BF)
            ag_id["n", 1, k] = ag_start(buf)

    def u_start():
        for k in range(CHUNKS):
            ag_id["u", k] = ag_start(r.u1.at[k])

    def b1a():
        rb = jnp.concatenate([r.rb[1, k, z, y] for k in range(CHUNKS)], 0)
        mg = dot_nt(rb, full[3].reshape(D, D))
        for k in range(CHUNKS):
            rows = slice(k * ROWS, (k + 1) * ROWS)
            m = mg[rows]
            cvg = m * r.proj1[1, rows]
            r.cv1[k, pl.ds(0, ROWS)] = cvg
            r.pbf1[rows, D : 2 * D] = (m * r.conv1[k]).astype(BF)
            slot = k - begin * (1 - c)

            def send(k=k, slot=slot):
                remote(
                    r.cv1.at[k, pl.ds(0, 8)], r.hg1b.at[slot], r.hg1send.at[k], r.hg1recv.at[slot], prev_dev
                ).start()

            if k == 0:
                pl.when(begin * (1 - c) == 0)(send)
            else:
                send()

    def b1b():
        taps = [0.0, 0.0, 0.0]
        for k in range(CHUNKS):

            def get(k=k):
                await_bytes(r.hg1b.at[k], r.hg1recv.at[k])

            def zero(k=k):
                r.hg1b[k] = jnp.zeros((8, D), F32)

            if k == CHUNKS - 1:
                none = end * c
                pl.when(none == 0)(get)
                pl.when(none == 1)(zero)
            else:
                get()
            e = r.cv1.at[k]
            e[pl.ds(ROWS, 8)] = r.hg1b[k]
            gg = sum(r.trow[2 - j : 3 - j] * e[pl.ds(j, ROWS)] for j in range(3))
            rows = slice(k * ROWS, (k + 1) * ROWS)
            r.pbf1[rows, :D] = (gg * r.proj1[2, rows]).astype(BF)
            r.pbf1[rows, 2 * D :] = (gg * r.proj1[0, rows]).astype(BF)
            cvg = e[pl.ds(0, ROWS)]
            for j in range(3):
                taps[j] = taps[j] + jnp.sum(cvg * r.gp1[k, pl.ds(6 + j, ROWS)], 0, keepdims=True)
        r.tap1g[...] = jnp.concatenate(taps, 0)
        wide = dot_nn(r.pbf1[...], full_in())
        for k in (1, 0):
            rows = r.rg[1, k] + wide[k * ROWS : (k + 1) * ROWS]
            r.g0own[k] = rows
            u = r.gbf.at[k]
            u[z, y] = rows.astype(BF)
            ag_id["g", k] = ag_start(u)
            emit(1, k, rows, r.ligst, r.ig, 1)

    def b1_exchange():
        for k in range(CHUNKS):
            ag_id["r", 1, k] = ag_start(r.rb.at[1, k])
        for i in range(NW):
            lanes = slice(i * LW, (i + 1) * LW)
            for p in range(3):
                r.pms[i, :, p * LW : (p + 1) * LW] = r.pbf1[:, p * D + i * LW : p * D + (i + 1) * LW]
            r.pms[i, :, 3 * LW :] = r.mixed1[:, lanes]
        mine = r.pm.at[w]
        mine[...] = r.pms[w]

        def it(i, carry):
            dev = wa_peer(i)
            remote(r.pms.at[dev[2]], mine, r.pmsem.at[0], r.pmsem.at[1], dev).start()
            return carry

        lax.fori_loop(1, NW, it, 0)

    X = [r.Xgu, r.Xdn, r.Xcv]
    Y = [r.Ygu, r.Ydn, r.Ycv]
    R = [r.Rgu, r.Rdn, r.Rcv]
    flush = [
        [(r.Ygu, r.o_gu)],
        [(r.Ydn, r.o_dn)],
        [(r.Ycv.at[pl.ds(0, 3 * LW)], r.o_in), (r.Ycv.at[pl.ds(3 * LW, LW)], r.o_out)],
    ]

    def flush_copies(i):
        return [
            pltpu.make_async_copy(src, dst, r.lsem.at[len(loads) + i + n]) for n, (src, dst) in enumerate(flush[i])
        ]

    by_row = [True, False, True]

    def part(ref, i, q):
        if by_row[i]:
            size = ref.shape[0] // NX
            return ref.at[pl.ds(pl.multiple_of(q * size, size), size)]
        size = ref.shape[1] // NX
        return ref.at[:, pl.ds(pl.multiple_of(q * size, size), size)]

    def w1(l):
        for n0, n in tiles(D):
            cols = slice(n0, n0 + n)
            for g in range(2):
                r.Xgu[l, g * HW : (g + 1) * HW, cols] = sum(
                    dot_tn(r.gub[l, k, :, g * HP : (g + 1) * HP], flat(r.norm.at[l, k], cols))
                    for k in range(CHUNKS)
                )[:HW].astype(BF)
        for n0, n in tiles(D):
            r.Xdn[l, :, n0 : n0 + n] = sum(
                dot_tn(
                    r.hid[l, k],
                    outbf(l, k)[:, n0 : n0 + n] if l == 1 else flat(outbf(l, k), slice(n0, n0 + n)),
                )
                for k in range(CHUNKS)
            )[:HW].astype(BF)

    def w2_0():
        for n0, n in tiles(D):
            cols = slice(n0, n0 + n)
            r.Xcv[0, : 3 * LW, cols] = sum(
                dot_tn(r.pbf[k], r.tok[k, :, cols]) for k in range(CHUNKS)
            ).astype(BF)
            r.Xcv[0, 3 * LW :, cols] = sum(
                dot_tn(r.mixed[k], flat(r.rb.at[0, k], cols)) for k in range(CHUNKS)
            ).astype(BF)

    def w2_1():
        await_bytes(r.pm.at[pl.ds(0, NW - 1)], r.pmsem.at[1])
        for k in range(CHUNKS):
            ag_wait(ag_id["u", k], r.u1.at[k])
            ag_wait(ag_id["r", 1, k], r.rb.at[1, k])
        pm = [r.pm[:, k * ROWS : (k + 1) * ROWS].reshape(T, 4 * LW) for k in range(CHUNKS)]
        for n0, n in tiles(D):
            cols = slice(n0, n0 + n)
            r.Xcv[1, : 3 * LW, cols] = sum(
                dot_tn(pm[k][:, : 3 * LW], flat(r.u1.at[k], cols)) for k in range(CHUNKS)
            ).astype(BF)
            r.Xcv[1, 3 * LW :, cols] = sum(
                dot_tn(pm[k][:, 3 * LW :], flat(r.rb.at[1, k], cols)) for k in range(CHUNKS)
            ).astype(BF)

    def core_send(l, i):
        @pl.when(c != l)
        def _():
            remote(X[i].at[l], Y[i], r.csend.at[i], r.crecv.at[i], core_peer).start()

    def x_reduce(l, i):
        @pl.when(c == l)
        def _():
            await_bytes(Y[i], r.crecv.at[i])
            rows_total = Y[i].shape[0]

            def add(rows):
                X[i][l, rows] = (X[i][l, rows].astype(F32) + Y[i][rows].astype(F32)).astype(BF)

            row_loop(rows_total, 32, add)
            mine = R[i].at[x]
            for j in range(1, NX):
                dev = x_peer(j)
                remote(
                    part(X[i].at[l], i, dev[1]), mine, r.xsend.at[i], r.xrecv.at[i], dev
                ).start()

    def x_gather(l, i):
        @pl.when(c == l)
        def _():
            await_bytes(R[i].at[pl.ds(0, NX - 1)], r.xrecv.at[i])
            src = part(X[i].at[l], i, x)
            R[i][x] = src[...]
            dst = part(Y[i], i, x)
            rows_total = dst.shape[0]

            def add(rows):
                total = R[i][0, rows].astype(F32)
                for j in range(1, NX):
                    total = total + R[i][j, rows].astype(F32)
                dst[rows] = total.astype(BF)

            row_loop(rows_total, 16, add)
            for j in range(1, NX):
                remote(dst, dst, r.vsend.at[i], r.vrecv.at[i], x_peer(j)).start()

    def x_finish(l, i):
        @pl.when(c == l)
        def _():
            await_bytes(R[i].at[pl.ds(0, NX - 1)], r.vrecv.at[i])
            await_bytes(R[i].at[pl.ds(0, NX - 1)], r.xsend.at[i])
            await_bytes(R[i].at[pl.ds(0, NX - 1)], r.vsend.at[i])
            for cp in flush_copies(i):
                cp.start()

        @pl.when(c != l)
        def _():
            await_bytes(Y[i], r.csend.at[i])

    GR = D // 128

    def gain_send(l):
        st = r.gst.at[l]
        for i in range(GR):
            st[0, i : i + 1] = r.gacc[l, :, i * 128 : (i + 1) * 128]
        gain = st[0, 0:GR]
        for i in range(NW):
            st[i, 0:GR] = gain
            st[i, GR:] = jnp.zeros((8, 128), F32)
            if l == 1:
                st[i, GR : GR + 3, :LW] = r.tap1g[:, i * LW : (i + 1) * LW]
        mine = r.gex.at[l, w]
        mine[...] = st[w]

        def it(i, carry):
            dev = wa_peer(i)
            remote(st.at[dev[2]], mine, r.gsend.at[l], r.grecv.at[l], dev).start()
            return carry

        lax.fori_loop(1, NW, it, 0)

    def gain_recv(l):
        await_bytes(r.gex.at[l, pl.ds(0, NW - 1)], r.grecv.at[l])
        total = r.gex[l, 0]
        for i in range(1, NW):
            total = total + r.gex[l, i]
        r.sm[l] = total

    def small_send(l):
        if l == 0:
            r.sm[0, GR:] = r.sm[0, GR:] + r.tacc[...]

        @pl.when(c != l)
        def _():
            remote(r.sm.at[l], r.smY, r.csend.at[3], r.crecv.at[3], core_peer).start()

    def small_x(l):
        @pl.when(c == l)
        def _():
            await_bytes(r.smY, r.crecv.at[3])
            mine = r.smR.at[x]
            mine[...] = r.sm[l] + r.smY[...]
            for j in range(1, NX):
                remote(mine, mine, r.xsend.at[3], r.xrecv.at[3], x_peer(j)).start()

    def small_finish(l):
        @pl.when(c == l)
        def _():
            await_bytes(r.smR.at[pl.ds(0, NX - 1)], r.xrecv.at[3])
            total = r.smR[0]
            for j in range(1, NX):
                total = total + r.smR[j]
            for i in range(GR):
                r.o_gain[:, i * 128 : (i + 1) * 128] = total[i : i + 1]
            r.o_tap[...] = total[GR : GR + 3, :LW]
            await_bytes(r.smR.at[pl.ds(0, NX - 1)], r.xsend.at[3])

        @pl.when(c != l)
        def _():
            await_bytes(r.smY, r.csend.at[3])

    A, B = 0, 1
    AB, BA = (0, 1), (1, 0)
    s1(0, A)
    s1(0, B)
    gather_wa()
    s2(0, A)
    s2(0, B)
    gather_mid()
    mids("rs", 0, "a", AB)
    gather_x(0)
    s3(0, A)
    s3(0, B)
    gather_x(1)
    mids("ag", 0, "n", AB)
    s4(0, A)
    s4_down(0, A)
    s4(0, B)
    s4_down(0, B)
    gather_x(2)
    prep_cot(A)
    mids("rs", 0, "b", AB)
    gather_core(0)
    gather_x(3)
    prep_cot(B)
    s5(0, A)
    s5(0, B)
    gather_core(1)
    f1a()
    gather_core(3)
    f1b()
    mids("ag", 1, "n", AB)
    u_start()
    s4(1, A)
    s4(1, B)
    t1(1, B)
    t1(1, A)
    mids("rs", 1, "c", BA)
    w1(1)
    t2(1, B)
    t2(1, A)
    mids("ag", 1, "u", AB)
    b1a()
    s4_down(1, A)
    s4_down(1, B)
    core_send(1, 0)
    core_send(1, 1)
    b1b()
    mids("ag", 0, "g", BA)
    gain_send(1)
    mids("rs", 1, "b", AB)
    b1_exchange()
    x_reduce(1, 0)
    x_reduce(1, 1)
    t1(0, B)
    t1(0, A)
    w1(0)
    core_send(0, 0)
    core_send(0, 1)
    s5(1, A)
    s5(1, B)
    mids("rs", 0, "c", BA)
    gain_recv(1)
    small_send(1)
    x_gather(1, 0)
    x_gather(1, 1)
    x_reduce(0, 0)
    x_reduce(0, 1)
    t2(0, B)
    t2(0, A)
    mids("ag", 0, "r", BA)
    gain_send(0)
    t3(0, B)
    t3(0, A)
    mids("ag", 1, "r", BA)
    x_gather(0, 0)
    x_gather(0, 1)
    t4(0, B)
    t4(0, A)
    w2_0()
    core_send(0, 2)
    w2_1()
    core_send(1, 2)
    mids("rs", 0, "d", BA)
    x_reduce(0, 2)
    gain_recv(0)
    small_send(0)
    small_x(0)
    x_reduce(1, 2)
    small_x(1)
    t5(0, B)
    t5(0, A)
    x_gather(1, 2)
    for i in range(3):
        x_finish(1, i)
    x_gather(0, 2)
    small_finish(1)
    for i in range(3):
        x_finish(0, i)
    small_finish(0)
    gather_close()
    await_bytes(r.pm.at[pl.ds(0, NW - 1)], r.pmsem.at[0])

    for sems, staging, target, out in ((0, r.lost, r.lo, r.o_layer), (1, r.ligst, r.ig, r.o_grad)):
        for k in range(CHUNKS):
            await_bytes(staging.at[0, k], r.orecv.at[sems, k])
            await_bytes(staging.at[0, k], r.osend.at[sems, k])
        out[...] = target[...]
    for n, buf in ag_sent:
        for i in range(2):
            await_bytes(ag_first(buf), r.ags.at[n, i])
            await_bytes(ag_second(buf), r.ags.at[n, 2 + i])
    for uses in stage_use:
        for n, buf in uses[-2:]:
            stage_sent(n, buf)
        for n, buf in uses:
            await_bytes(r.rwa.at[n, pl.ds(0, NZ - 1)], r.rss.at[n, 2])
            await_bytes(r.rwb.at[n, pl.ds(0, NY - 1)], r.rss.at[n, 3])
    for l in range(2):
        await_bytes(r.gex.at[l, pl.ds(0, NW - 1)], r.gsend.at[l])
    for fsem, fbuf, bsem, bbuf, no_next, no_prev in (
        (r.hsend, r.hs, r.hgsend, r.hgs, last * c, first * (1 - c)),
        (r.h1send, r.h1s, r.hg1send, r.hg1b, end * c, begin * (1 - c)),
    ):
        for k in range(CHUNKS):

            def fwd(k=k, fsem=fsem, fbuf=fbuf):
                await_bytes(fbuf.at[k], fsem.at[k])

            def bwd(k=k, bsem=bsem, bbuf=bbuf):
                await_bytes(bbuf.at[k], bsem.at[k])

            if k == CHUNKS - 1:
                pl.when(no_next == 0)(fwd)
            else:
                fwd()
            if k == 0:
                pl.when(no_prev == 0)(bwd)
            else:
                bwd()
    for cp in wcopies:
        cp.wait_send()
    for i in range(3):
        for cp in flush_copies(i):
            cp.wait()


def body(NX, NW, tokens, cotangent, in_weight, conv_weight, out_weight, norm_gain, gate_up_weight, down_weight):
    micro, T, D = tokens.shape
    LW = conv_weight.shape[2]
    HW = gate_up_weight.shape[3]
    HP = -(-HW // 128) * 128
    GR = D // 128
    L, K = 2, CHUNKS
    vmem = pltpu.VMEM
    dma = pltpu.SemaphoreType.DMA
    n_ag, n_rs = 6 * K, 6 * K
    NY = NZ = next(i for i in range(1, NW + 1) if i * i >= NW)
    plane = (NZ, NY, ROWS, D)
    ins = dict(
        tokens=tokens, cotangent=cotangent, w_in=in_weight[0].transpose(1, 2, 0), w_out=out_weight[0],
        w_gu=gate_up_weight[0].transpose(1, 2, 0), w_dn=down_weight[0],
        w_gain=norm_gain, w_conv=conv_weight.transpose(1, 0, 2)
    )
    anyspec = pl.BlockSpec(memory_space=pl.ANY)
    vspec = pl.BlockSpec(memory_space=pltpu.VMEM)
    shape = jax.ShapeDtypeStruct
    outs = dict(
        o_layer=(shape((micro, ROWS, D), BF), vspec),
        o_grad=(shape((micro, ROWS, D), F32), vspec),
        o_in=(shape((3 * LW, D), BF), anyspec),
        o_out=(shape((LW, D), BF), anyspec),
        o_gu=(shape((2 * HW, D), BF), anyspec),
        o_dn=(shape((HW, D), BF), anyspec),
        o_gain=(shape((1, D), F32), vspec),
        o_tap=(shape((3, LW), F32), vspec),
    )
    scratch = dict(
        Cown=vmem((L, 4, LW, D), BF), Cfull=vmem((4, NZ, NY, LW, D), BF),
        Wgu=vmem((L, 2, HP, D), BF), Wdn=vmem((L, HP, D), BF), Wsm=vmem((L, 8, D), F32),
        tok=vmem((K, T, D), BF), cot=vmem((K, T, D), F32), cotb=vmem((K, T, D), BF),
        projB=vmem((K, T, LW), F32), projC=vmem((K, T, LW), F32), projX=vmem((K, T, LW), F32),
        gp=vmem((K, T + 8, LW), F32), conv=vmem((K, T, LW), F32), mixed=vmem((K, T, LW), BF),
        gu=vmem((L, K, T, 2 * HP), F32), hg=vmem((K, T, HP), F32), hid=vmem((L, K, T, HP), BF),
        gub=vmem((L, K, T, 2 * HP), BF), pbf=vmem((K, T, 3 * LW), BF),
        res=vmem((L, K, ROWS, D), F32), rg=vmem((L, K, ROWS, D), F32), g0own=vmem((K, ROWS, D), F32),
        cvg=vmem((K, T + 8, LW), F32),
        norm=vmem((L, K) + plane, BF), u1=vmem((K,) + plane, BF), rb=vmem((L, K) + plane, BF), gbf=vmem((K,) + plane, BF),
        stage=vmem((K, 2) + plane, BF), rva=vmem((n_rs, NY, NZ, ROWS, D // 2), BF), rvb=vmem((n_rs, NZ, NY, ROWS, D // 2), BF),
        rsa=vmem((n_rs, NZ, ROWS, D // 2), BF), rsb=vmem((n_rs, NY, ROWS, D // 2), BF),
        rwa=vmem((n_rs, NZ, ROWS, D // 2), BF), rwb=vmem((n_rs, NY, ROWS, D // 2), BF),
        hs=vmem((K, 16, LW), BF), hb=vmem((K, 16, LW), BF), hgs=vmem((K, 8, LW), F32), hgb=vmem((K, 8, LW), F32),
        proj1=vmem((3, K * ROWS, D), F32), gp1=vmem((K, ROWS + 8, D), F32), conv1=vmem((K, ROWS, D), F32),
        mixed1=vmem((K * ROWS, D), BF), cv1=vmem((K, ROWS + 8, D), F32), pbf1=vmem((K * ROWS, 3 * D), BF),
        h1s=vmem((K, ROWS, D), BF), h1b=vmem((K, ROWS, D), BF), hg1b=vmem((K, 8, D), F32),
        trow=vmem((3, D), F32), tap1g=vmem((3, D), F32), taps1=vmem((NW, 8, 128), F32),
        pms=vmem((NW, K * ROWS, 4 * LW), BF), pm=vmem((NW, K * ROWS, 4 * LW), BF),
        lost=vmem((L, K, ROWS, D), BF), ligst=vmem((L, K, ROWS, D), F32),
        lo=vmem((micro, ROWS, D), BF), ig=vmem((micro, ROWS, D), F32),
        Xgu=vmem((L, 2 * HW, D), BF), Xdn=vmem((L, HW, D), BF), Xcv=vmem((L, 4 * LW, D), BF),
        Ygu=vmem((2 * HW, D), BF), Ydn=vmem((HW, D), BF), Ycv=vmem((4 * LW, D), BF),
        Rgu=vmem((NX, 2 * HW // NX, D), BF), Rdn=vmem((NX, HW, D // NX), BF), Rcv=vmem((NX, 4 * LW // NX, D), BF),
        gacc=vmem((L, 1, D), F32), tacc=vmem((8, 128), F32), gst=vmem((L, NW, GR + 8, 128), F32),
        gex=vmem((L, NW, GR + 8, 128), F32), sm=vmem((L, GR + 8, 128), F32),
        smY=vmem((GR + 8, 128), F32), smR=vmem((NX, GR + 8, 128), F32),
        lsem=dma((16,)), wsend=dma((5,)), wrecv=dma((5,)), ags=dma((n_ag, 4)), agr=dma((n_ag, 4)),
        rss=dma((n_rs, 4)), rsr=dma((n_rs, 4)), hsend=dma((K,)), hrecv=dma((K,)), hgsend=dma((K,)), hgrecv=dma((K,)),
        h1send=dma((K,)), h1recv=dma((K,)), hg1send=dma((K,)), hg1recv=dma((K,)), pmsem=dma((2,)),
        gwsem=dma((11,)), gxs=dma((4,)), gxr=dma((4,)), gcs=dma((4,)), gcr=dma((4,)),
        osend=dma((2, K)), orecv=dma((2, K)), csend=dma((4,)), crecv=dma((4,)), xsend=dma((4,)), xrecv=dma((4,)),
        vsend=dma((3,)), vrecv=dma((3,)), gsend=dma((L,)), grecv=dma((L,)),
    )
    names = tuple(ins) + tuple(outs) + tuple(scratch)
    layer, grad, g_in, g_out, g_gu, g_dn, g_gain, g_tap = pl.pallas_call(
        functools.partial(kernel, (NX, NW, T, D, LW, HW, HP), names),
        out_shape=tuple(o[0] for o in outs.values()),
        in_specs=[anyspec] * (len(ins) - 2) + [vspec] * 2,
        out_specs=tuple(o[1] for o in outs.values()),
        scratch_shapes=list(scratch.values()),
        compiler_params=pltpu.CompilerParams(
            collective_id=0, has_side_effects=True, vmem_limit_bytes=63 << 20
        ),
    )(*ins.values())
    return (
        layer[None],
        grad[None],
        g_in.reshape(3, LW, D).transpose(2, 0, 1).astype(F32)[None],
        g_tap[None],
        g_out.astype(F32)[None],
        g_gain,
        g_gu.reshape(2, HW, D).transpose(2, 0, 1).astype(F32)[None],
        g_dn.astype(F32)[None],
    )


def solution(mesh):
    in_specs = (
        P(None, "seq", None),
        P(None, "seq", None),
        P("section", None, None, "wa"),
        P("section", None, "wa"),
        P("section", "wa", None),
        P("section", None),
        P("section", None, None, "wa"),
        P("section", "wa", None),
    )
    out_specs = (
        P("section", None, ("seq", "wa"), None),
        P("section", None, ("seq", "wa"), None),
        P("section", None, None, "wa"),
        P("section", None, "wa"),
        P("section", "wa", None),
        P("section", None),
        P("section", None, None, "wa"),
        P("section", "wa", None),
    )
    fn = functools.partial(body, mesh.shape["seq"], mesh.shape["wa"])
    return jax.shard_map(fn, mesh=mesh, in_specs=in_specs, out_specs=out_specs, check_vma=False)
```
